32 devices in a mesh: slab: 4 (over y, x), ctrl: 8 (over z, core).
Axes of the slice: x: 2, y: 2, z: 4, core: 2. Of those that a mesh axis runs over, the one named last changes fastest.
Arguments:
- value: float32 [64, 128, 128], P('slab'), may hold values from -6 to 6
- speed: float32 [64, 128, 128], P('slab'), may hold values from 0.25 to 1
- reward: bfloat16 [16, 64, 128, 128], P('ctrl', 'slab'), may hold values from -0.8984375 to 0.8984375
- ctrl_set: int32 [16], P('ctrl'), may hold values from 0 to 15, as said below
- drift_sets: float32 [16, 3], replicated, may hold values from -0.08 to 0.08
- diffusion_sets: float32 [16, 3], replicated, may hold values from 0.03 to 0.12
Outputs:
- value_out: float32 [64, 128, 128], P('slab')
The draws below stay inside these ranges and needn't reach their ends.
Inputs may be any that keep to these rules, and one draw needn't show every extreme that they name: `ctrl_set`: each of the 16 sets is named by exactly 1 controls.
All inputs are finite; a program needn't handle non-finite values.
Results may differ from the reference program's by a relative error of at most 0.0014.
Values may be sent and summed in bfloat16 or wider, within the bound.
No kernel may reach another device: no remote copies, remote signals or barrier semaphores. Data moves between devices by JAX's collectives and lax.ppermute only.
A program may use at most 64 MiB of HBM per device.

```python
import jax
import jax.numpy as jnp
from jax import lax

NY = 128
NZ = 128
SETS = 16
SUBSTEPS = 3
OUTER = 2
NX = 64
CONTROLS = 16


def draw_ctrl_set(key, part):
    return (jax.random.permutation(jax.random.fold_in(key, 7), CONTROLS) % SETS).astype(jnp.int32)


def block_scale(own_key, extent, cuts, smallest, largest):
    loudness, own = 1.0, jax.random.fold_in(own_key, 6)
    for dim, parts in cuts:
        draws = jnp.exp(jax.random.uniform(jax.random.fold_in(own, dim), (parts,), jnp.float32, smallest / len(cuts), largest / len(cuts)))
        loudness = loudness * jnp.repeat(draws, extent[dim] // parts).reshape([-1 if axis == dim else 1 for axis in range(len(extent))])
    return loudness


def normal_values(own_key, dims, spread, bound, shards=(), kind=jnp.bfloat16):
    array = jax.random.normal(own_key, dims, jnp.float32) * spread
    if len(shards) > 0:
        array = block_scale(own_key, dims, shards, -0.22, 0.18) * array
    return jnp.clip(array, min=-bound, max=bound).astype(kind)


def setup_inputs(seed: int = 0) -> dict:
    arg_keys = jax.random.split(jax.random.key(seed), 7)
    return {
        "value": normal_values(arg_keys[0], (NX, NY, NZ), 1.0, 6.0, ((0, 4),), jnp.float32),
        "speed": jnp.clip(0.25 + 0.75 * jax.random.uniform(arg_keys[1], (NX, NY, NZ), jnp.float32) ** block_scale(arg_keys[1], (NX, NY, NZ), ((0, 4),), -0.2, 0.2), 0.25, 1.0),
        "reward": normal_values(arg_keys[2], (CONTROLS, NX, NY, NZ), 0.15, 0.8984375, ((0, 8), (1, 4))),
        "ctrl_set": draw_ctrl_set(jax.random.fold_in(arg_keys[6], 71), 0),
        "drift_sets": jnp.clip(jax.random.uniform(arg_keys[4], (SETS, 3), jnp.float32, -0.08, 0.08), -0.08, 0.08),
        "diffusion_sets": jnp.clip(jax.random.uniform(arg_keys[5], (SETS, 3), jnp.float32, 0.03, 0.12), 0.03, 0.12),
    }


def upshift(field, axis):
    widths = [(0, 0)] * 4
    widths[axis] = (0, 1)
    padded = jnp.pad(field, widths)
    return lax.slice_in_dim(padded, 1, padded.shape[axis], axis=axis)


def downshift(field, axis):
    widths = [(0, 0)] * 4
    widths[axis] = (1, 0)
    padded = jnp.pad(field, widths)
    return lax.slice_in_dim(padded, 0, padded.shape[axis] - 1, axis=axis)


def advance(padded, speed_part, reward_part, diffusion, drift):
    center = padded[:, 1:-1]
    ahead = [padded[:, 2:], upshift(center, 2), upshift(center, 3)]
    behind = [padded[:, :-2], downshift(center, 2), downshift(center, 3)]
    total = center + reward_part
    for axis_num in range(3):
        rate = diffusion[:, axis_num][:, None, None, None]
        flow = drift[:, axis_num][:, None, None, None] * speed_part[None]
        forward = ahead[axis_num] - center
        backward = center - behind[axis_num]
        total = total + rate * (forward - backward) + jnp.maximum(flow, 0.0) * forward + jnp.minimum(flow, 0.0) * backward
    return total


def reference(value, speed, reward, ctrl_set, drift_sets, diffusion_sets):
    diffusion = diffusion_sets[ctrl_set]
    drift = drift_sets[ctrl_set]
    current = value
    for outer_round in range(OUTER):
        def visit(best, inputs):
            reward_one, diffusion_one, drift_one = inputs
            field = current[None]
            for substep in range(SUBSTEPS):
                padded = jnp.pad(field, ((0, 0), (1, 1), (0, 0), (0, 0)))
                field = advance(padded, speed, reward_one.astype(jnp.float32)[None], diffusion_one[None], drift_one[None])
            return jnp.maximum(best, field[0]), None

        start = jnp.full(current.shape, -jnp.inf, dtype=current.dtype)
        current, unused = lax.scan(visit, start, (reward, diffusion, drift))
    return current
```

```python
import functools

import jax
import jax.numpy as jnp
from jax import lax
from jax.experimental import pallas as pl
from jax.experimental.pallas import tpu as pltpu
from jax.sharding import PartitionSpec as P

SUBSTEPS = 3
OUTER = 2
PAD = 8
LOWEST = -3.0e38
COEFS = 12


def mate(chip, step, chips):
    if chips & (chips - 1) == 0:
        return chip ^ step
    return (chip + step) % chips


def shift_rows(rows, count, start):
    return lax.dynamic_slice_in_dim(rows, start, count, axis=0)


def stencil(coef, ctrl, src, row, first, size, speed, reward, fixed):
    lines = pl.ds(PAD + first, size)
    center = src[row, lines, :]
    y_ahead = src[row, pl.ds(PAD + first + 1, size), :]
    y_behind = src[row, pl.ds(PAD + first - 1, size), :]
    x_sum = src[row + 1, lines, :] + src[row - 1, lines, :]
    x_wind = src[row + fixed["x_step"], lines, :]
    depth = center.shape[1]
    lane = lax.broadcasted_iota(jnp.int32, center.shape, 1)
    z_ahead = jnp.where(lane == depth - 1, 0.0, pltpu.roll(center, depth - 1, 1))
    z_behind = jnp.where(lane == 0, 0.0, pltpu.roll(center, 1, 1))
    y_wind = jnp.where(fixed["y_up"], y_ahead, y_behind)
    z_wind = jnp.where(fixed["z_up"], z_ahead, z_behind)
    still = reward + coef[ctrl, 6] * center + coef[ctrl, 0] * x_sum
    still = still + coef[ctrl, 1] * (y_ahead + y_behind) + coef[ctrl, 2] * (z_ahead + z_behind)
    wind = coef[ctrl, 3] * x_wind + coef[ctrl, 4] * y_wind + coef[ctrl, 5] * z_wind
    return still + speed * (wind - coef[ctrl, 7] * center)


def march(place, coef, block, speed, reward, out, mid, late, chips, half, ny):
    lines = out.shape[1]
    chunk = min(lines, ny)
    count = reward.shape[0]
    chip = place[0]
    low = place[1].astype(jnp.float32)
    high = place[2].astype(jnp.float32)
    for shard in range(chips):
        out[shard] = jnp.full(out.shape[1:], LOWEST, out.dtype)

    def one(ctrl, carry):
        fixed = {
            "x_step": jnp.where(coef[ctrl, 8] > 0.0, 1, -1),
            "y_up": coef[ctrl, 9] > 0.0,
            "z_up": coef[ctrl, 10] > 0.0,
        }
        fields = [block, mid, late]
        for substep in range(SUBSTEPS):
            last = substep == SUBSTEPS - 1
            for row in range(substep + 1, half + 2 * SUBSTEPS - 1 - substep):
                for first in range(0, ny, chunk):
                    part = pl.ds(first, chunk)
                    new = stencil(
                        coef,
                        ctrl,
                        fields[substep],
                        row,
                        first,
                        chunk,
                        speed[row - 1, part, :],
                        reward[ctrl, row - 1, part, :],
                        fixed,
                    )
                    if last:
                        line = (row - SUBSTEPS) * ny + first
                        shard = mate(chip, line // lines, chips)
                        spot = pl.ds(line % lines, chunk)
                        out[shard, spot, :] = jnp.maximum(out[shard, spot, :], new)
                    else:
                        if row < SUBSTEPS:
                            new = new * low
                        if row >= SUBSTEPS + half:
                            new = new * high
                        fields[substep + 1][row, pl.ds(PAD + first, chunk), :] = new
        return carry

    lax.fori_loop(0, count, one, 0)


def clear_pads(fields, ny):
    for field in fields:
        zero = jnp.zeros((PAD, field.shape[2]), field.dtype)
        for row in range(field.shape[0]):
            field[row, 0:PAD, :] = zero
            field[row, PAD + ny : 2 * PAD + ny, :] = zero


def lay_out(place, speed, reward, other, edge, edge_own, speed_ext, reward_ext, half):
    core = place[3]
    margin = SUBSTEPS - 1
    own = reward.shape[0]
    inner = half + margin
    head = margin * (1 - core)
    tail = inner * core
    start = (half - margin) * core
    for row in range(inner):
        speed_ext[row + head] = speed[row + start]
        for ctrl in range(own):
            reward_ext[ctrl, row + head] = reward[ctrl, row + start].astype(jnp.float32)
            reward_ext[own + ctrl, row + head] = other[ctrl, row].astype(jnp.float32)
    for row in range(margin):
        speed_ext[row + tail] = edge[SUBSTEPS + row].astype(jnp.float32)
        for ctrl in range(own):
            reward_ext[ctrl, row + tail] = edge_own[ctrl * margin + row].astype(jnp.float32)
            reward_ext[own + ctrl, row + tail] = edge[
                SUBSTEPS + margin + ctrl * margin + row
            ].astype(jnp.float32)


def first_kernel(
    place, coef, value, speed, reward, other, edge, edge_own, out, block, mid, late, speed_ext, reward_ext, *, chips
):
    half = speed_ext.shape[0] - 2 * (SUBSTEPS - 1)
    ny = value.shape[1]
    core = place[3]
    clear_pads((block, mid, late), ny)
    middle = pl.ds(PAD, ny)
    inner = half + SUBSTEPS
    for row in range(inner):
        block[row + SUBSTEPS * (1 - core), middle, :] = value[row + (half - SUBSTEPS) * core]
    for row in range(SUBSTEPS):
        block[row + inner * core, middle, :] = edge[row].astype(jnp.float32)
    lay_out(place, speed, reward, other, edge, edge_own, speed_ext, reward_ext, half)
    march(place, coef, block, speed_ext, reward_ext, out, mid, late, chips, half, ny)


def second_kernel(
    place, coef, current, below, above, speed, reward, other, edge, edge_own, out, block, mid, late, speed_ext, reward_ext, *, chips
):
    half = speed_ext.shape[0] - 2 * (SUBSTEPS - 1)
    ny = below.shape[1]
    lines = current.shape[1]
    chunk = min(lines, ny)
    clear_pads((block, mid, late), ny)
    middle = pl.ds(PAD, ny)
    for row in range(SUBSTEPS):
        block[row, middle, :] = below[row]
        block[SUBSTEPS + half + row, middle, :] = above[row]
    for line in range(0, half * ny, chunk):
        row, first = line // ny, line % ny
        block[SUBSTEPS + row, pl.ds(PAD + first, chunk), :] = current[
            mate(place[0], line // lines, chips), pl.ds(line % lines, chunk), :
        ]
    lay_out(place, speed, reward, other, edge, edge_own, speed_ext, reward_ext, half)
    march(place, coef, block, speed_ext, reward_ext, out, mid, late, chips, half, ny)


def run_kernel(kernel, chips, half, count, ny, nz, place, coef, arrays):
    lines = half * ny // chips
    padded = pltpu.VMEM((half + 2 * SUBSTEPS, ny + 2 * PAD, nz), jnp.float32)
    inner = half + 2 * (SUBSTEPS - 1)
    cells = count * nz * ny * (3 * half + SUBSTEPS * (SUBSTEPS - 1))
    return pl.pallas_call(
        functools.partial(kernel, chips=chips),
        out_shape=jax.ShapeDtypeStruct((chips, lines, nz), jnp.float32),
        in_specs=[pl.BlockSpec(memory_space=pltpu.SMEM)] * 2
        + [pl.BlockSpec(memory_space=pltpu.VMEM)] * len(arrays),
        out_specs=pl.BlockSpec(memory_space=pltpu.VMEM),
        scratch_shapes=[
            padded,
            padded,
            padded,
            pltpu.VMEM((inner, ny, nz), jnp.float32),
            pltpu.VMEM((count, inner, ny, nz), jnp.float32),
        ],
        compiler_params=pltpu.CompilerParams(vmem_limit_bytes=32 * 2**20),
        cost_estimate=pl.CostEstimate(flops=25 * cells, bytes_accessed=4 * 2**20, transcendentals=0),
    )(place, coef, *arrays)


def body(value, speed, reward, ctrl_set, drift_sets, diffusion_sets):
    own, cells, ny, nz = reward.shape
    slabs, members = lax.axis_size("slab"), lax.axis_size("ctrl")
    chips, half = members // 2, cells // 2
    slab, member = lax.axis_index("slab"), lax.axis_index("ctrl")
    chip, core = member // 2, member % 2
    margin = SUBSTEPS - 1
    narrow = jnp.bfloat16

    def device(s, z, c):
        return s * members + 2 * z + c

    partners = [(i, i ^ 1) for i in range(members)]
    across, along = [], []
    for s in range(slabs - 1):
        for z in range(chips):
            across += [(device(s, z, 1), device(s + 1, z, 0)), (device(s + 1, z, 0), device(s, z, 1))]
            along += [(device(s, z, 0), device(s + 1, z, 0)), (device(s + 1, z, 1), device(s, z, 1))]

    other_set = lax.ppermute(ctrl_set, "ctrl", partners)
    other = lax.ppermute(
        lax.dynamic_slice_in_dim(reward, (half - margin) * (1 - core), half + margin, axis=1), "ctrl", partners
    )
    near = core * (cells - margin)
    rim = jnp.concatenate(
        [
            shift_rows(value, SUBSTEPS, core * (cells - SUBSTEPS)).astype(narrow),
            shift_rows(speed, margin, near).astype(narrow),
            lax.dynamic_slice_in_dim(reward, near, margin, axis=1).reshape(own * margin, ny, nz),
        ],
        axis=0,
    )
    edge = lax.ppermute(rim, ("slab", "ctrl"), across)
    far = lax.dynamic_slice_in_dim(reward, (1 - core) * (cells - margin), margin, axis=1)
    edge_own = lax.ppermute(far.reshape(own * margin, ny, nz), ("slab", "ctrl"), along)

    sets = jnp.concatenate([ctrl_set, other_set])
    picked = sets[:, None] == jnp.arange(drift_sets.shape[0], dtype=jnp.int32)[None, :]
    diffusion = jnp.sum(jnp.where(picked[:, :, None], diffusion_sets[None], 0.0), axis=1)
    drift = jnp.sum(jnp.where(picked[:, :, None], drift_sets[None], 0.0), axis=1)
    size = jnp.abs(drift)
    coef = jnp.concatenate(
        [
            diffusion,
            size,
            1.0 - 2.0 * jnp.sum(diffusion, axis=1, keepdims=True),
            jnp.sum(size, axis=1, keepdims=True),
            drift,
            jnp.zeros((2 * own, 1), jnp.float32),
        ],
        axis=1,
    )
    place = jnp.stack(
        [
            chip,
            jnp.where((slab == 0) & (core == 0), 0, 1),
            jnp.where((slab == slabs - 1) & (core == 1), 0, 1),
            core,
        ]
    ).astype(jnp.int32)
    run = functools.partial(run_kernel, chips=chips, half=half, count=2 * own, ny=ny, nz=nz, place=place, coef=coef)
    shared = (speed, reward, other, edge, edge_own)

    def merge(best):
        wire = best.astype(jnp.float16)
        mine = wire[0]
        for step in range(1, chips):
            pairs = [(2 * z + c, 2 * mate(z, step, chips) + c) for z in range(chips) for c in range(2)]
            mine = jnp.maximum(mine, lax.ppermute(wire[step], "ctrl", pairs))
        pieces = [mine]
        for step in range(1, chips):
            pairs = [(2 * mate(z, step, chips) + c, 2 * z + c) for z in range(chips) for c in range(2)]
            pieces.append(lax.ppermute(mine, "ctrl", pairs))
        return pieces

    def in_order(pieces):
        stacked = jnp.stack(pieces)
        return jnp.concatenate(
            [lax.dynamic_index_in_dim(stacked, mate(chip, shard, chips), 0, keepdims=False) for shard in range(chips)]
            if chips & (chips - 1) == 0
            else [
                lax.dynamic_index_in_dim(stacked, (shard - chip) % chips, 0, keepdims=False) for shard in range(chips)
            ]
        ).reshape(half, ny, nz)

    pieces = merge(run(first_kernel, arrays=(value,) + shared))
    for _ in range(1, OUTER):
        rows = in_order(pieces)
        bottom, top = rows[:SUBSTEPS], rows[half - SUBSTEPS :]
        from_core = lax.ppermute(jnp.where(core == 0, top, bottom), "ctrl", partners).astype(jnp.float32)
        from_slab = lax.ppermute(jnp.where(core == 0, bottom, top), ("slab", "ctrl"), across).astype(jnp.float32)
        below = jnp.where(core == 0, from_slab, from_core)
        above = jnp.where(core == 0, from_core, from_slab)
        current = jnp.stack(pieces).astype(jnp.float32)
        pieces = merge(run(second_kernel, arrays=(current, below, above) + shared))
    rows = in_order(pieces)
    partner_rows = lax.ppermute(rows, "ctrl", partners)
    lower = jnp.where(core == 0, rows, partner_rows).astype(jnp.float32)
    upper = jnp.where(core == 0, partner_rows, rows).astype(jnp.float32)
    return jnp.concatenate([lower, upper], axis=0)


def solution(mesh):
    in_specs = (
        P("slab", None, None),
        P("slab", None, None),
        P("ctrl", "slab", None, None),
        P("ctrl"),
        P(),
        P(),
    )
    out_specs = P("slab", None, None)
    return jax.shard_map(body, mesh=mesh, in_specs=in_specs, out_specs=out_specs, check_vma=False)
```

```python
import functools

import jax
import jax.numpy as jnp
from jax import lax
from jax.experimental import pallas as pl
from jax.experimental.pallas import tpu as pltpu
from jax.sharding import PartitionSpec as P

SUBSTEPS = 3
PAD = 8
LOWEST = -3.0e38


def mate(chip, step, chips):
    if chips & (chips - 1) == 0:
        return chip ^ step
    return (chip + step) % chips


def mate_step(chip, other, chips):
    if chips & (chips - 1) == 0:
        return chip ^ other
    return (other - chip) % chips


def stencil(coef, ctrl, src, row, speed, reward, winds):
    ny = src.shape[1] - 2 * PAD
    lines = pl.ds(PAD, ny)
    center = src[row, lines, :]
    y_ahead = src[row, pl.ds(PAD + 1, ny), :]
    y_behind = src[row, pl.ds(PAD - 1, ny), :]
    x_sum = src[row + 1, lines, :] + src[row - 1, lines, :]
    x_wind = src[row + winds[0], lines, :]
    nz = center.shape[1]
    lane = lax.broadcasted_iota(jnp.int32, center.shape, 1)
    z_ahead = jnp.where(lane == nz - 1, 0.0, pltpu.roll(center, nz - 1, 1))
    z_behind = jnp.where(lane == 0, 0.0, pltpu.roll(center, 1, 1))
    y_wind = jnp.where(winds[1], y_ahead, y_behind)
    z_wind = jnp.where(winds[2], z_ahead, z_behind)
    still = reward + coef[ctrl, 6] * center + coef[ctrl, 0] * x_sum
    still = still + coef[ctrl, 1] * (y_ahead + y_behind) + coef[ctrl, 2] * (z_ahead + z_behind)
    wind = coef[ctrl, 3] * x_wind + coef[ctrl, 4] * y_wind + coef[ctrl, 5] * z_wind
    return still + speed * (wind - coef[ctrl, 7] * center)


def winds_of(place, coef, ctrl):
    step = jnp.where(coef[ctrl, 8] > 0.0, 1, -1)
    return jnp.where(place[1] == 0, step, -step), coef[ctrl, 9] > 0.0, coef[ctrl, 10] > 0.0


def put_max(place, out, index, new):
    chips, width = out.shape[0], out.shape[2]
    for shard in range(chips):
        spot = mate_step(place[0], shard, chips)
        out[spot, index] = jnp.maximum(out[spot, index], new[shard * width : (shard + 1) * width])


def start_max(out):
    for shard in range(out.shape[0]):
        for row in range(out.shape[1]):
            out[shard, row] = jnp.full(out.shape[2:], LOWEST, out.dtype)


def clear_pads(field, ny):
    zero = jnp.zeros((PAD, field.shape[2]), field.dtype)
    for row in range(field.shape[0]):
        field[row, 0:PAD, :] = zero
        field[row, PAD + ny : 2 * PAD + ny, :] = zero


def lay_own(place, first, last, base, speed, reward, other, speed_rows, reward_rows):
    cells = speed.shape[0]
    own = reward.shape[0]
    for row in range(first, last):
        real = jnp.where(place[1] == 0, row, cells - 1 - row)
        speed_rows[row - base] = speed[real]
        for ctrl in range(own):
            reward_rows[ctrl, row - base] = reward[ctrl, real].astype(jnp.float32)
            reward_rows[own + ctrl, row - base] = other[ctrl, real].astype(jnp.float32)


def lay_edge(base, edge, edge_own, speed_rows, reward_rows):
    margin = SUBSTEPS - 1
    own = edge_own.shape[0] // margin
    for row in range(margin):
        spot = -1 - row - base
        speed_rows[spot] = edge[SUBSTEPS + row].astype(jnp.float32)
        for ctrl in range(own):
            reward_rows[ctrl, spot] = edge_own[ctrl * margin + row].astype(jnp.float32)
            far = edge[SUBSTEPS + margin + ctrl * margin + row]
            reward_rows[own + ctrl, spot] = far.astype(jnp.float32)


def spread(place, pieces, index, field, row):
    chips, width = pieces.shape[0], pieces.shape[2]
    for shard in range(chips):
        piece = pieces[mate_step(place[0], shard, chips), index]
        field[row, pl.ds(PAD + shard * width, width), :] = piece.astype(field.dtype)


def early_march(place, coef, known, half, block, speed_rows, reward_rows, out, keeps, fields):
    ny = block.shape[1] - 2 * PAD
    start_max(out)

    def one(ctrl, carry):
        winds = winds_of(place, coef, ctrl)
        source = block
        for substep in range(SUBSTEPS):
            for q in range(known + 1 + substep, half + SUBSTEPS - 1 - substep):
                row = q - known
                new = stencil(coef, ctrl, source, row, speed_rows[row], reward_rows[ctrl, row], winds)
                if substep == SUBSTEPS - 1:
                    put_max(place, out, q - known - SUBSTEPS, new)
                    continue
                fields[substep][row, pl.ds(PAD, ny), :] = new
                if row < substep + 3:
                    keeps[substep][ctrl, row - substep - 1] = new
            if substep < SUBSTEPS - 1:
                source = fields[substep]
        return carry

    lax.fori_loop(0, reward_rows.shape[0], one, 0)


def rest_march(place, coef, known, block, speed_rows, reward_rows, out, keeps, fields):
    ny = block.shape[1] - 2 * PAD
    inside = place[2].astype(jnp.float32)
    start_max(out)

    def one(ctrl, carry):
        winds = winds_of(place, coef, ctrl)
        source = block
        for substep in range(SUBSTEPS):
            for q in range(substep + 1 - SUBSTEPS, known + 1 + substep):
                given = q + SUBSTEPS - 1
                new = stencil(
                    coef, ctrl, source, q + SUBSTEPS, speed_rows[given], reward_rows[ctrl, given], winds
                )
                if substep == SUBSTEPS - 1:
                    put_max(place, out, q, new)
                    continue
                if q < 0:
                    new = new * inside
                fields[substep][q + SUBSTEPS, pl.ds(PAD, ny), :] = new
            if substep < SUBSTEPS - 1:
                source = fields[substep]
                for kept in range(2):
                    row = known + 1 + substep + kept + SUBSTEPS
                    source[row, pl.ds(PAD, ny), :] = keeps[substep][ctrl, kept]
        return carry

    lax.fori_loop(0, reward_rows.shape[0], one, 0)


def pack_kernel(place, value, speed, reward, edge, far):
    cells = value.shape[0]
    own = reward.shape[0]
    margin = SUBSTEPS - 1
    for row in range(SUBSTEPS):
        near = jnp.where(place[1] == 0, row, cells - 1 - row)
        away = jnp.where(place[1] == 0, cells - 1 - row, row)
        edge[row] = value[near].astype(edge.dtype)
        if row < margin:
            edge[SUBSTEPS + row] = speed[near].astype(edge.dtype)
            for ctrl in range(own):
                edge[SUBSTEPS + margin + ctrl * margin + row] = reward[ctrl, near]
                far[ctrl * margin + row] = reward[ctrl, away]


def early_first(place, coef, value, speed, reward, other, out, *refs, half):
    keeps, fields, (block, speed_rows, reward_rows) = refs[:2], refs[2:4], refs[4:]
    cells, ny = value.shape[:2]
    for field in (block, *fields):
        clear_pads(field, ny)
    for q in range(half + SUBSTEPS):
        block[q, pl.ds(PAD, ny), :] = value[jnp.where(place[1] == 0, q, cells - 1 - q)]
    lay_own(place, 1, half + SUBSTEPS - 1, 0, speed, reward, other, speed_rows, reward_rows)
    early_march(place, coef, 0, half, block, speed_rows, reward_rows, out, keeps, fields)


def rest_first(place, coef, value, speed, reward, other, edge, edge_own, *refs, half):
    keeps, out, fields, (block, speed_rows, reward_rows) = refs[:2], refs[2], refs[3:5], refs[5:]
    cells, ny = value.shape[:2]
    for field in (block, *fields):
        clear_pads(field, ny)
    for q in range(-SUBSTEPS, 2):
        if q < 0:
            block[q + SUBSTEPS, pl.ds(PAD, ny), :] = edge[-1 - q].astype(jnp.float32)
        else:
            block[q + SUBSTEPS, pl.ds(PAD, ny), :] = value[jnp.where(place[1] == 0, q, cells - 1 - q)]
    lay_edge(1 - SUBSTEPS, edge, edge_own, speed_rows, reward_rows)
    lay_own(place, 0, SUBSTEPS, 1 - SUBSTEPS, speed, reward, other, speed_rows, reward_rows)
    rest_march(place, coef, 0, block, speed_rows, reward_rows, out, keeps, fields)


def early_later(place, coef, inner, across, speed, reward, other, out, *refs, half):
    keeps, fields, (block, speed_rows, reward_rows) = refs[:2], refs[2:4], refs[4:]
    ny = speed.shape[1]
    for field in (block, *fields):
        clear_pads(field, ny)
    for q in range(SUBSTEPS, half):
        spread(place, inner, q - SUBSTEPS, block, q - SUBSTEPS)
    for row in range(SUBSTEPS):
        spread(place, across, SUBSTEPS - 1 - row, block, half + row - SUBSTEPS)
    lay_own(place, SUBSTEPS + 1, half + SUBSTEPS - 1, SUBSTEPS, speed, reward, other, speed_rows, reward_rows)
    early_march(place, coef, SUBSTEPS, half, block, speed_rows, reward_rows, out, keeps, fields)


def rest_later(place, coef, inner, outer, beyond, speed, reward, other, edge, edge_own, *refs, half):
    keeps, out, fields, (block, speed_rows, reward_rows) = refs[:2], refs[2], refs[3:5], refs[5:]
    ny = speed.shape[1]
    for field in (block, *fields):
        clear_pads(field, ny)
    for row in range(SUBSTEPS):
        spread(place, beyond, row, block, SUBSTEPS - 1 - row)
        spread(place, outer, row, block, SUBSTEPS + row)
    for row in range(2):
        spread(place, inner, row, block, 2 * SUBSTEPS + row)
    lay_edge(1 - SUBSTEPS, edge, edge_own, speed_rows, reward_rows)
    lay_own(place, 0, 2 * SUBSTEPS, 1 - SUBSTEPS, speed, reward, other, speed_rows, reward_rows)
    rest_march(place, coef, SUBSTEPS, block, speed_rows, reward_rows, out, keeps, fields)


def body(value, speed, reward, ctrl_set, drift_sets, diffusion_sets):
    own, cells, ny, nz = reward.shape
    count = 2 * own
    slabs, members = lax.axis_size("slab"), lax.axis_size("ctrl")
    chips, half = members // 2, cells // 2
    width = ny // chips
    slab, member = lax.axis_index("slab"), lax.axis_index("ctrl")
    chip, core = member // 2, member % 2
    margin = SUBSTEPS - 1
    narrow, wire = jnp.bfloat16, jnp.float16
    both = ("slab", "ctrl")

    def device(s, z, c):
        return s * members + 2 * z + c

    partners = [(i, i ^ 1) for i in range(members)]

    def facing(step):
        pairs = []
        for s in range(slabs - 1):
            for z in range(chips):
                to = mate(z, step, chips)
                pairs += [(device(s, to, 1), device(s + 1, z, 0)), (device(s + 1, to, 0), device(s, z, 1))]
        return pairs

    along = []
    for s in range(slabs - 1):
        for z in range(chips):
            along += [(device(s, z, 0), device(s + 1, z, 0)), (device(s + 1, z, 1), device(s, z, 1))]

    whole = pl.BlockSpec(memory_space=pltpu.VMEM)
    scalars = pl.BlockSpec(memory_space=pltpu.SMEM)
    place = jnp.stack(
        [
            chip,
            core,
            jnp.where(slab == jnp.where(core == 0, 0, slabs - 1), 0, 1),
        ]
    ).astype(jnp.int32)

    def shape(*dims, kind=jnp.float32):
        return jax.ShapeDtypeStruct(dims, kind)

    def call(kernel, rows, first, arrays, outs):
        field = pltpu.VMEM((rows, ny + 2 * PAD, nz), jnp.float32)
        return pl.pallas_call(
            functools.partial(kernel, half=half),
            out_shape=outs,
            in_specs=[scalars] * 2 + [whole] * len(arrays),
            out_specs=jax.tree.map(lambda _: whole, outs),
            scratch_shapes=[
                field,
                field,
                field,
                pltpu.VMEM((rows, ny, nz), jnp.float32),
                pltpu.VMEM((count, rows, ny, nz), jnp.float32),
            ],
            compiler_params=pltpu.CompilerParams(vmem_limit_bytes=32 * 2**20),
            cost_estimate=pl.CostEstimate(
                flops=25 * count * first * ny * nz, bytes_accessed=2**20, transcendentals=0
            ),
        )(place, coef, *arrays)

    keeps = [shape(count, 2, ny, nz)] * (SUBSTEPS - 1)

    other_set = lax.ppermute(ctrl_set, "ctrl", partners)
    other = lax.ppermute(reward, "ctrl", partners)
    edge_rows = SUBSTEPS + margin + own * margin
    packed, far = pl.pallas_call(
        pack_kernel,
        out_shape=[shape(edge_rows, ny, nz, kind=narrow), shape(own * margin, ny, nz, kind=narrow)],
        in_specs=[scalars] + [whole] * 3,
        out_specs=[whole] * 2,
    )(place, value, speed, reward)
    edge = lax.ppermute(packed, both, facing(0))
    edge_own = lax.ppermute(far, both, along)

    sets = jnp.concatenate([ctrl_set, other_set])
    picked = sets[:, None] == jnp.arange(drift_sets.shape[0], dtype=jnp.int32)[None, :]
    diffusion = jnp.sum(jnp.where(picked[:, :, None], diffusion_sets[None], 0.0), axis=1)
    drift = jnp.sum(jnp.where(picked[:, :, None], drift_sets[None], 0.0), axis=1)
    size = jnp.abs(drift)
    coef = jnp.concatenate(
        [
            diffusion,
            size,
            1.0 - 2.0 * jnp.sum(diffusion, axis=1, keepdims=True),
            jnp.sum(size, axis=1, keepdims=True),
            drift,
            jnp.zeros((count, 1), jnp.float32),
        ],
        axis=1,
    )

    def reduce(best):
        parts = best.astype(wire)
        mine = parts[0]
        for step in range(1, chips):
            pairs = [(2 * z + c, 2 * mate(z, step, chips) + c) for z in range(chips) for c in range(2)]
            mine = jnp.maximum(mine, lax.ppermute(parts[step], "ctrl", pairs))
        return mine

    def gather(mine):
        pieces = [mine]
        for step in range(1, chips):
            pairs = [(2 * mate(z, step, chips) + c, 2 * z + c) for z in range(chips) for c in range(2)]
            pieces.append(lax.ppermute(mine, "ctrl", pairs))
        return jnp.stack(pieces)

    steps = sum(half + SUBSTEPS - 2 - 2 * k for k in range(SUBSTEPS))
    best, *kept = call(
        early_first,
        half + SUBSTEPS,
        steps,
        (value, speed, reward, other),
        [shape(chips, half - SUBSTEPS, width, nz)] + keeps,
    )
    inner_mine = reduce(best)
    best = call(
        rest_first,
        2 * SUBSTEPS + 2,
        SUBSTEPS * SUBSTEPS,
        (value, speed, reward, other, edge, edge_own, *kept),
        shape(chips, SUBSTEPS, width, nz),
    )
    inner = gather(inner_mine)
    across = lax.ppermute(inner[:, -SUBSTEPS:], "ctrl", partners)
    outer_mine = reduce(best)
    outer = gather(outer_mine)
    beyond = jnp.stack([lax.ppermute(outer_mine, both, facing(step)) for step in range(chips)])

    inner_full = inner.astype(jnp.float32)
    best_early, *kept = call(
        early_later,
        half,
        steps - SUBSTEPS * SUBSTEPS,
        (inner_full, across.astype(jnp.float32), speed, reward, other),
        [shape(chips, half - 2 * SUBSTEPS, width, nz)] + keeps,
    )
    best_rest = call(
        rest_later,
        3 * SUBSTEPS + 2,
        2 * SUBSTEPS * SUBSTEPS,
        (
            inner_full,
            outer.astype(jnp.float32),
            beyond.astype(jnp.float32),
            speed,
            reward,
            other,
            edge,
            edge_own,
            *kept,
        ),
        shape(chips, 2 * SUBSTEPS, width, nz),
    )
    pieces = gather(reduce(jnp.concatenate([best_rest, best_early], axis=1)))

    from_partner = lax.ppermute(pieces, "ctrl", partners)
    lower = jnp.where(core == 0, pieces, from_partner)
    upper = jnp.where(core == 0, from_partner, pieces)[:, ::-1]
    slab_pieces = jnp.concatenate([lower, upper], axis=1)
    ordered = [
        lax.dynamic_index_in_dim(slab_pieces, mate_step(chip, shard, chips), 0, keepdims=False)
        for shard in range(chips)
    ]
    return jnp.concatenate(ordered, axis=1).astype(jnp.float32)


def solution(mesh):
    in_specs = (
        P("slab", None, None),
        P("slab", None, None),
        P("ctrl", "slab", None, None),
        P("ctrl"),
        P(),
        P(),
    )
    out_specs = P("slab", None, None)
    return jax.shard_map(body, mesh=mesh, in_specs=in_specs, out_specs=out_specs, check_vma=False)
```

```python
import functools

import jax
import jax.numpy as jnp
from jax import lax
from jax.experimental import pallas as pl
from jax.experimental.pallas import tpu as pltpu
from jax.sharding import PartitionSpec as P

SUBSTEPS = 3
PAD = 8
LOWEST = -3.0e38


def mate(chip, step, chips):
    if chips & (chips - 1) == 0:
        return chip ^ step
    return (chip + step) % chips


def mate_step(chip, other, chips):
    if chips & (chips - 1) == 0:
        return chip ^ other
    return (other - chip) % chips


def stencil(coef, ctrl, src, row, speed, reward, winds):
    ny = src.shape[1] - 2 * PAD
    lines = pl.ds(PAD, ny)
    center = src[row, lines, :]
    y_ahead = src[row, pl.ds(PAD + 1, ny), :]
    y_behind = src[row, pl.ds(PAD - 1, ny), :]
    x_sum = src[row + 1, lines, :] + src[row - 1, lines, :]
    x_wind = src[row + winds[0], lines, :]
    nz = center.shape[1]
    lane = lax.broadcasted_iota(jnp.int32, center.shape, 1)
    z_ahead = jnp.where(lane == nz - 1, 0.0, pltpu.roll(center, nz - 1, 1))
    z_behind = jnp.where(lane == 0, 0.0, pltpu.roll(center, 1, 1))
    y_wind = jnp.where(winds[1], y_ahead, y_behind)
    z_wind = jnp.where(winds[2], z_ahead, z_behind)
    still = reward + coef[ctrl, 6] * center + coef[ctrl, 0] * x_sum
    still = still + coef[ctrl, 1] * (y_ahead + y_behind) + coef[ctrl, 2] * (z_ahead + z_behind)
    wind = coef[ctrl, 3] * x_wind + coef[ctrl, 4] * y_wind + coef[ctrl, 5] * z_wind
    return still + speed * (wind - coef[ctrl, 7] * center)


def winds_of(place, coef, ctrl):
    step = jnp.where(coef[ctrl, 8] > 0.0, 1, -1)
    return jnp.where(place[1] == 0, step, -step), coef[ctrl, 9] > 0.0, coef[ctrl, 10] > 0.0


def put_max(place, out, index, new):
    chips, width = out.shape[0], out.shape[2]
    for shard in range(chips):
        spot = mate_step(place[0], shard, chips)
        out[spot, index] = jnp.maximum(out[spot, index], new[shard * width : (shard + 1) * width])


def start_max(out):
    for shard in range(out.shape[0]):
        for row in range(out.shape[1]):
            out[shard, row] = jnp.full(out.shape[2:], LOWEST, out.dtype)


def clear_pads(field, ny):
    zero = jnp.zeros((PAD, field.shape[2]), field.dtype)
    for row in range(field.shape[0]):
        field[row, 0:PAD, :] = zero
        field[row, PAD + ny : 2 * PAD + ny, :] = zero


def lay_own(place, first, last, base, speed, reward, other, speed_rows, reward_rows):
    cells = speed.shape[0]
    own = reward.shape[0]
    for row in range(first, last):
        real = jnp.where(place[1] == 0, row, cells - 1 - row)
        speed_rows[row - base] = speed[real]
        for ctrl in range(own):
            reward_rows[ctrl, row - base] = reward[ctrl, real].astype(jnp.float32)
            reward_rows[own + ctrl, row - base] = other[ctrl, real].astype(jnp.float32)


def lay_edge(base, edge, edge_own, speed_rows, reward_rows):
    margin = SUBSTEPS - 1
    own = edge_own.shape[0] // margin
    for row in range(margin):
        spot = -1 - row - base
        speed_rows[spot] = edge[SUBSTEPS + row].astype(jnp.float32)
        for ctrl in range(own):
            reward_rows[ctrl, spot] = edge_own[ctrl * margin + row].astype(jnp.float32)
            far = edge[SUBSTEPS + margin + ctrl * margin + row]
            reward_rows[own + ctrl, spot] = far.astype(jnp.float32)


def spread(place, pieces, index, field, row):
    chips, width = pieces.shape[0], pieces.shape[2]
    for shard in range(chips):
        piece = pieces[mate_step(place[0], shard, chips), index]
        field[row, pl.ds(PAD + shard * width, width), :] = piece.astype(field.dtype)


def early_march(place, coef, known, half, block, speed_rows, reward_rows, out, keeps, fields):
    ny = block.shape[1] - 2 * PAD
    start_max(out)

    def one(ctrl, carry):
        winds = winds_of(place, coef, ctrl)
        source = block
        for substep in range(SUBSTEPS):
            for q in range(known + 1 + substep, half + SUBSTEPS - 1 - substep):
                row = q - known
                new = stencil(coef, ctrl, source, row, speed_rows[row], reward_rows[ctrl, row], winds)
                if substep == SUBSTEPS - 1:
                    put_max(place, out, q - known - SUBSTEPS, new)
                    continue
                fields[substep][row, pl.ds(PAD, ny), :] = new
                if row < substep + 3:
                    keeps[substep][ctrl, row - substep - 1] = new
            if substep < SUBSTEPS - 1:
                source = fields[substep]
        return carry

    lax.fori_loop(0, reward_rows.shape[0], one, 0)


def rest_march(place, coef, known, block, speed_rows, reward_rows, out, keeps, fields):
    ny = block.shape[1] - 2 * PAD
    inside = place[2].astype(jnp.float32)
    start_max(out)

    def one(ctrl, carry):
        winds = winds_of(place, coef, ctrl)
        source = block
        for substep in range(SUBSTEPS):
            for q in range(substep + 1 - SUBSTEPS, known + 1 + substep):
                given = q + SUBSTEPS - 1
                new = stencil(
                    coef, ctrl, source, q + SUBSTEPS, speed_rows[given], reward_rows[ctrl, given], winds
                )
                if substep == SUBSTEPS - 1:
                    put_max(place, out, q, new)
                    continue
                if q < 0:
                    new = new * inside
                fields[substep][q + SUBSTEPS, pl.ds(PAD, ny), :] = new
            if substep < SUBSTEPS - 1:
                source = fields[substep]
                for kept in range(2):
                    row = known + 1 + substep + kept + SUBSTEPS
                    source[row, pl.ds(PAD, ny), :] = keeps[substep][ctrl, kept]
        return carry

    lax.fori_loop(0, reward_rows.shape[0], one, 0)


def pack_kernel(place, value, speed, reward, edge, far, value_rows, speed_rows, value_sem, speed_sem, near_sem, far_sem):
    cells = value.shape[0]
    own = reward.shape[0]
    margin = SUBSTEPS - 1
    copies, later = [], []
    for row in range(SUBSTEPS):
        near = jnp.where(place[1] == 0, row, cells - 1 - row)
        away = jnp.where(place[1] == 0, cells - 1 - row, row)
        copies.append(pltpu.make_async_copy(value.at[near], value_rows.at[row], value_sem.at[row]))
        if row < margin:
            copies.append(pltpu.make_async_copy(speed.at[near], speed_rows.at[row], speed_sem.at[row]))
            for ctrl in range(own):
                spot = ctrl * margin + row
                place_near = edge.at[SUBSTEPS + margin + spot]
                later.append(pltpu.make_async_copy(reward.at[ctrl, near], place_near, near_sem.at[spot]))
                later.append(pltpu.make_async_copy(reward.at[ctrl, away], far.at[spot], far_sem.at[spot]))
    for copy in copies + later:
        copy.start()
    for copy in copies:
        copy.wait()
    for row in range(SUBSTEPS):
        edge[row] = value_rows[row].astype(edge.dtype)
    for row in range(margin):
        edge[SUBSTEPS + row] = speed_rows[row].astype(edge.dtype)
    for copy in later:
        copy.wait()


def early_first(place, coef, value, speed, reward, other, out, *refs, half):
    keeps, fields, (block, speed_rows, reward_rows) = refs[:2], refs[2:4], refs[4:]
    cells, ny = value.shape[:2]
    for field in (block, *fields):
        clear_pads(field, ny)
    for q in range(half + SUBSTEPS):
        block[q, pl.ds(PAD, ny), :] = value[jnp.where(place[1] == 0, q, cells - 1 - q)]
    lay_own(place, 1, half + SUBSTEPS - 1, 0, speed, reward, other, speed_rows, reward_rows)
    early_march(place, coef, 0, half, block, speed_rows, reward_rows, out, keeps, fields)


def rest_first(place, coef, value, speed, reward, other, edge, edge_own, *refs, half):
    keeps, out, fields, (block, speed_rows, reward_rows) = refs[:2], refs[2], refs[3:5], refs[5:]
    cells, ny = value.shape[:2]
    for field in (block, *fields):
        clear_pads(field, ny)
    for q in range(-SUBSTEPS, 2):
        if q < 0:
            block[q + SUBSTEPS, pl.ds(PAD, ny), :] = edge[-1 - q].astype(jnp.float32)
        else:
            block[q + SUBSTEPS, pl.ds(PAD, ny), :] = value[jnp.where(place[1] == 0, q, cells - 1 - q)]
    lay_edge(1 - SUBSTEPS, edge, edge_own, speed_rows, reward_rows)
    lay_own(place, 0, SUBSTEPS, 1 - SUBSTEPS, speed, reward, other, speed_rows, reward_rows)
    rest_march(place, coef, 0, block, speed_rows, reward_rows, out, keeps, fields)


def early_later(place, coef, current, across, speed, reward, other, out, *refs, half):
    keeps, fields, (block, speed_rows, reward_rows) = refs[:2], refs[2:4], refs[4:]
    ny = speed.shape[1]
    for field in (block, *fields):
        clear_pads(field, ny)
    for q in range(half):
        spread(place, current, q, block, q)
    for row in range(SUBSTEPS):
        spread(place, across, SUBSTEPS - 1 - row, block, half + row)
    lay_own(place, 1, half + SUBSTEPS - 1, 0, speed, reward, other, speed_rows, reward_rows)
    early_march(place, coef, 0, half, block, speed_rows, reward_rows, out, keeps, fields)


def rest_later(place, coef, current, beyond, speed, reward, other, edge, edge_own, *refs, half):
    keeps, out, fields, (block, speed_rows, reward_rows) = refs[:2], refs[2], refs[3:5], refs[5:]
    ny = speed.shape[1]
    for field in (block, *fields):
        clear_pads(field, ny)
    for row in range(SUBSTEPS):
        spread(place, beyond, row, block, SUBSTEPS - 1 - row)
    for row in range(2):
        spread(place, current, row, block, SUBSTEPS + row)
    lay_edge(1 - SUBSTEPS, edge, edge_own, speed_rows, reward_rows)
    lay_own(place, 0, SUBSTEPS, 1 - SUBSTEPS, speed, reward, other, speed_rows, reward_rows)
    rest_march(place, coef, 0, block, speed_rows, reward_rows, out, keeps, fields)


def body(value, speed, reward, ctrl_set, drift_sets, diffusion_sets):
    own, cells, ny, nz = reward.shape
    count = 2 * own
    slabs, members = lax.axis_size("slab"), lax.axis_size("ctrl")
    chips, half = members // 2, cells // 2
    width = ny // chips
    slab, member = lax.axis_index("slab"), lax.axis_index("ctrl")
    chip, core = member // 2, member % 2
    margin = SUBSTEPS - 1
    narrow, wire = jnp.bfloat16, jnp.float16
    both = ("slab", "ctrl")

    def device(s, z, c):
        return s * members + 2 * z + c

    partners = [(i, i ^ 1) for i in range(members)]

    def facing(step):
        pairs = []
        for s in range(slabs - 1):
            for z in range(chips):
                to = mate(z, step, chips)
                pairs += [(device(s, to, 1), device(s + 1, z, 0)), (device(s + 1, to, 0), device(s, z, 1))]
        return pairs

    along = []
    for s in range(slabs - 1):
        for z in range(chips):
            along += [(device(s, z, 0), device(s + 1, z, 0)), (device(s + 1, z, 1), device(s, z, 1))]

    whole = pl.BlockSpec(memory_space=pltpu.VMEM)
    scalars = pl.BlockSpec(memory_space=pltpu.SMEM)
    place = jnp.stack(
        [
            chip,
            core,
            jnp.where(slab == jnp.where(core == 0, 0, slabs - 1), 0, 1),
        ]
    ).astype(jnp.int32)

    def shape(*dims, kind=jnp.float32):
        return jax.ShapeDtypeStruct(dims, kind)

    def call(kernel, rows, first, arrays, outs):
        field = pltpu.VMEM((rows, ny + 2 * PAD, nz), jnp.float32)
        return pl.pallas_call(
            functools.partial(kernel, half=half),
            out_shape=outs,
            in_specs=[scalars] * 2 + [whole] * len(arrays),
            out_specs=jax.tree.map(lambda _: whole, outs),
            scratch_shapes=[
                field,
                field,
                field,
                pltpu.VMEM((rows, ny, nz), jnp.float32),
                pltpu.VMEM((count, rows, ny, nz), jnp.float32),
            ],
            compiler_params=pltpu.CompilerParams(vmem_limit_bytes=32 * 2**20),
            cost_estimate=pl.CostEstimate(
                flops=25 * count * first * ny * nz, bytes_accessed=2**20, transcendentals=0
            ),
        )(place, coef, *arrays)

    keeps = [shape(count, 2, ny, nz)] * (SUBSTEPS - 1)

    other_set = lax.ppermute(ctrl_set, "ctrl", partners)
    other = lax.ppermute(reward, "ctrl", partners)
    edge_rows = SUBSTEPS + margin + own * margin
    dma = pltpu.SemaphoreType.DMA
    packed, far = pl.pallas_call(
        pack_kernel,
        out_shape=[shape(edge_rows, ny, nz, kind=narrow), shape(own * margin, ny, nz, kind=narrow)],
        in_specs=[scalars] + [pl.BlockSpec(memory_space=pl.ANY)] * 3,
        out_specs=[whole] * 2,
        scratch_shapes=[
            pltpu.VMEM((SUBSTEPS, ny, nz), jnp.float32),
            pltpu.VMEM((margin, ny, nz), jnp.float32),
            dma((SUBSTEPS,)),
            dma((margin,)),
            dma((own * margin,)),
            dma((own * margin,)),
        ],
    )(place, value, speed, reward)
    edge = lax.ppermute(packed, both, facing(0))
    edge_own = lax.ppermute(far, both, along)

    sets = jnp.concatenate([ctrl_set, other_set])
    picked = sets[:, None] == jnp.arange(drift_sets.shape[0], dtype=jnp.int32)[None, :]
    diffusion = jnp.sum(jnp.where(picked[:, :, None], diffusion_sets[None], 0.0), axis=1)
    drift = jnp.sum(jnp.where(picked[:, :, None], drift_sets[None], 0.0), axis=1)
    size = jnp.abs(drift)
    coef = jnp.concatenate(
        [
            diffusion,
            size,
            1.0 - 2.0 * jnp.sum(diffusion, axis=1, keepdims=True),
            jnp.sum(size, axis=1, keepdims=True),
            drift,
            jnp.zeros((count, 1), jnp.float32),
        ],
        axis=1,
    )

    def reduce(best):
        parts = best.astype(wire)
        mine = parts[0]
        for step in range(1, chips):
            pairs = [(2 * z + c, 2 * mate(z, step, chips) + c) for z in range(chips) for c in range(2)]
            mine = jnp.maximum(mine, lax.ppermute(parts[step], "ctrl", pairs))
        return mine

    def gather(mine):
        pieces = [mine]
        for step in range(1, chips):
            pairs = [(2 * mate(z, step, chips) + c, 2 * z + c) for z in range(chips) for c in range(2)]
            pieces.append(lax.ppermute(mine, "ctrl", pairs))
        return jnp.stack(pieces)

    steps = sum(half + SUBSTEPS - 2 - 2 * k for k in range(SUBSTEPS))
    best, *kept = call(
        early_first,
        half + SUBSTEPS,
        steps,
        (value, speed, reward, other),
        [shape(chips, half - SUBSTEPS, width, nz)] + keeps,
    )
    best_rest = call(
        rest_first,
        2 * SUBSTEPS + 2,
        SUBSTEPS * SUBSTEPS,
        (value, speed, reward, other, edge, edge_own, *kept),
        shape(chips, SUBSTEPS, width, nz),
    )
    pieces = gather(reduce(jnp.concatenate([best_rest, best], axis=1)))

    across = lax.ppermute(pieces[:, -SUBSTEPS:], "ctrl", partners)
    beyond = lax.ppermute(pieces[:, :SUBSTEPS], both, facing(0))
    current = pieces.astype(jnp.float32)
    best, *kept = call(
        early_later,
        half + SUBSTEPS,
        steps,
        (current, across.astype(jnp.float32), speed, reward, other),
        [shape(chips, half - SUBSTEPS, width, nz)] + keeps,
    )
    best_rest = call(
        rest_later,
        2 * SUBSTEPS + 2,
        SUBSTEPS * SUBSTEPS,
        (current, beyond.astype(jnp.float32), speed, reward, other, edge, edge_own, *kept),
        shape(chips, SUBSTEPS, width, nz),
    )
    pieces = gather(reduce(jnp.concatenate([best_rest, best], axis=1)))

    from_partner = lax.ppermute(pieces, "ctrl", partners)
    lower = jnp.where(core == 0, pieces, from_partner)
    upper = jnp.where(core == 0, from_partner, pieces)[:, ::-1]
    slab_pieces = jnp.concatenate([lower, upper], axis=1)
    ordered = [
        lax.dynamic_index_in_dim(slab_pieces, mate_step(chip, shard, chips), 0, keepdims=False)
        for shard in range(chips)
    ]
    return jnp.concatenate(ordered, axis=1).astype(jnp.float32)


def solution(mesh):
    in_specs = (
        P("slab", None, None),
        P("slab", None, None),
        P("ctrl", "slab", None, None),
        P("ctrl"),
        P(),
        P(),
    )
    out_specs = P("slab", None, None)
    return jax.shard_map(body, mesh=mesh, in_specs=in_specs, out_specs=out_specs, check_vma=False)
```

```python
import functools

import jax
import jax.numpy as jnp
from jax import lax
from jax.experimental import pallas as pl
from jax.experimental.pallas import tpu as pltpu
from jax.sharding import PartitionSpec as P

SUBSTEPS = 3
PAD = 8
LOWEST = -3.0e38


def mate(chip, step, chips):
    if chips & (chips - 1) == 0:
        return chip ^ step
    return (chip + step) % chips


def mate_step(chip, other, chips):
    if chips & (chips - 1) == 0:
        return chip ^ other
    return (other - chip) % chips


def where_am_i():
    slab, member = lax.axis_index("slab"), lax.axis_index("ctrl")
    upper = (member + slab) % 2
    end = jnp.where(upper == 0, 0, lax.axis_size("slab") - 1)
    return member // 2, upper, jnp.where(slab == end, 0, 1)


def coefficients(sets, ctrl):
    own_set, other_set, drift_sets, diffusion_sets = sets
    own = own_set.shape[0]
    kind = jnp.where(ctrl < own, own_set[jnp.minimum(ctrl, own - 1)], other_set[jnp.maximum(ctrl - own, 0)])
    rates = [diffusion_sets[kind, dim] for dim in range(3)]
    drifts = [drift_sets[kind, dim] for dim in range(3)]
    sizes = [jnp.maximum(drift, -drift) for drift in drifts]
    return rates, sizes, 1.0 - 2.0 * (rates[0] + rates[1] + rates[2]), sizes[0] + sizes[1] + sizes[2], drifts


def stencil(coef, src, row, speed, reward, winds):
    ny = src.shape[1] - 2 * PAD
    lines = pl.ds(PAD, ny)
    center = src[row, lines, :]
    y_ahead = src[row, pl.ds(PAD + 1, ny), :]
    y_behind = src[row, pl.ds(PAD - 1, ny), :]
    x_sum = src[row + 1, lines, :] + src[row - 1, lines, :]
    x_wind = src[row + winds[0], lines, :]
    nz = center.shape[1]
    lane = lax.broadcasted_iota(jnp.int32, center.shape, 1)
    z_ahead = jnp.where(lane == nz - 1, 0.0, pltpu.roll(center, nz - 1, 1))
    z_behind = jnp.where(lane == 0, 0.0, pltpu.roll(center, 1, 1))
    y_wind = jnp.where(winds[1], y_ahead, y_behind)
    z_wind = jnp.where(winds[2], z_ahead, z_behind)
    rates, sizes, weight, size, _ = coef
    still = reward + weight * center + rates[0] * x_sum
    still = still + rates[1] * (y_ahead + y_behind) + rates[2] * (z_ahead + z_behind)
    wind = sizes[0] * x_wind + sizes[1] * y_wind + sizes[2] * z_wind
    return still + speed * (wind - size * center)


def winds_of(place, drifts):
    step = jnp.where(drifts[0] > 0.0, 1, -1)
    return jnp.where(place[1] == 0, step, -step), drifts[1] > 0.0, drifts[2] > 0.0


def put_max(place, out, index, new):
    chips, width = out.shape[0], out.shape[2]
    for shard in range(chips):
        spot = mate_step(place[0], shard, chips)
        out[spot, index] = jnp.maximum(out[spot, index], new[shard * width : (shard + 1) * width])


def start_max(out):
    for shard in range(out.shape[0]):
        for row in range(out.shape[1]):
            out[shard, row] = jnp.full(out.shape[2:], LOWEST, out.dtype)


def clear_pads(field, ny):
    zero = jnp.zeros((PAD, field.shape[2]), field.dtype)
    for row in range(field.shape[0]):
        field[row, 0:PAD, :] = zero
        field[row, PAD + ny : 2 * PAD + ny, :] = zero


def lay_rows(place, speed, reward, other, speed_rows, reward_rows):
    own, cells = reward.shape[:2]
    for q in range(speed_rows.shape[0]):
        real = jnp.where(place[1] == 0, q, cells - 1 - q)
        speed_rows[q] = speed[real]
        for ctrl in range(own):
            reward_rows[ctrl, q] = reward[ctrl, real].astype(jnp.float32)
            reward_rows[own + ctrl, q] = other[ctrl, real].astype(jnp.float32)


def lay_lower(edge, edge_other, lower_rows):
    mine = edge_other.shape[0]
    for row in range(mine):
        lower_rows[row] = edge[edge.shape[0] - mine + row]
        lower_rows[mine + row] = edge_other[row]


def spread(place, pieces, index, field, row):
    chips, width = pieces.shape[0], pieces.shape[2]
    for shard in range(chips):
        piece = pieces[mate_step(place[0], shard, chips), index]
        field[row, pl.ds(PAD + shard * width, width), :] = piece.astype(field.dtype)


def early_march(place, sets, half, block, speed_rows, reward_rows, out, keeps, fields):
    ny = block.shape[1] - 2 * PAD
    start_max(out)

    def one(ctrl, carry):
        coef = coefficients(sets, ctrl)
        winds = winds_of(place, coef[4])
        source = block
        for substep in range(SUBSTEPS):
            for q in range(1 + substep, half + SUBSTEPS - 1 - substep):
                new = stencil(coef, source, q, speed_rows[q], reward_rows[ctrl, q], winds)
                if substep == SUBSTEPS - 1:
                    put_max(place, out, q - SUBSTEPS, new)
                    continue
                fields[substep][q, pl.ds(PAD, ny), :] = new
                if q < substep + 3:
                    keeps[substep][ctrl, q - substep - 1] = new
            if substep < SUBSTEPS - 1:
                source = fields[substep]
        return carry

    lax.fori_loop(0, reward_rows.shape[0], one, 0)


def rest_march(place, sets, edge, lower_rows, block, speed_rows, reward_rows, out, keeps, fields):
    ny = block.shape[1] - 2 * PAD
    margin = SUBSTEPS - 1
    inside = place[2].astype(jnp.float32)
    start_max(out)

    def one(ctrl, carry):
        coef = coefficients(sets, ctrl)
        winds = winds_of(place, coef[4])
        source = block
        for substep in range(SUBSTEPS):
            for q in range(substep + 1 - SUBSTEPS, 1 + substep):
                if q < 0:
                    speed = edge[SUBSTEPS - 1 - q].astype(jnp.float32)
                    reward = lower_rows[ctrl * margin - 1 - q].astype(jnp.float32)
                else:
                    speed, reward = speed_rows[q], reward_rows[ctrl, q]
                new = stencil(coef, source, q + SUBSTEPS, speed, reward, winds)
                if substep == SUBSTEPS - 1:
                    put_max(place, out, q, new)
                    continue
                if q < 0:
                    new = new * inside
                fields[substep][q + SUBSTEPS, pl.ds(PAD, ny), :] = new
            if substep < SUBSTEPS - 1:
                source = fields[substep]
                for kept in range(2):
                    row = 1 + substep + kept + SUBSTEPS
                    source[row, pl.ds(PAD, ny), :] = keeps[substep][ctrl, kept]
        return carry

    lax.fori_loop(0, reward_rows.shape[0], one, 0)


def pack_kernel(value, speed, reward, edge, far, block, speed_rows, value_sem, speed_sem, near_sem, far_sem):
    place = where_am_i()
    cells, ny = value.shape[:2]
    own = reward.shape[0]
    margin = SUBSTEPS - 1
    copies, later = [], []
    for row in range(SUBSTEPS):
        near = jnp.where(place[1] == 0, row, cells - 1 - row)
        away = jnp.where(place[1] == 0, cells - 1 - row, row)
        copies.append(pltpu.make_async_copy(value.at[near], block.at[row, pl.ds(PAD, ny)], value_sem.at[row]))
        if row < margin:
            copies.append(pltpu.make_async_copy(speed.at[near], speed_rows.at[row], speed_sem.at[row]))
            for ctrl in range(own):
                spot = ctrl * margin + row
                place_near = edge.at[SUBSTEPS + margin + spot]
                later.append(pltpu.make_async_copy(reward.at[ctrl, near], place_near, near_sem.at[spot]))
                later.append(pltpu.make_async_copy(reward.at[ctrl, away], far.at[spot], far_sem.at[spot]))
    for row in range(SUBSTEPS, block.shape[0]):
        real = jnp.where(place[1] == 0, row, cells - 1 - row)
        later.append(pltpu.make_async_copy(value.at[real], block.at[row, pl.ds(PAD, ny)], value_sem.at[row]))
    for copy in copies + later:
        copy.start()
    clear_pads(block, ny)
    for copy in copies:
        copy.wait()
    for row in range(SUBSTEPS):
        edge[row] = block[row, pl.ds(PAD, ny), :].astype(edge.dtype)
    for row in range(margin):
        edge[SUBSTEPS + row] = speed_rows[row].astype(edge.dtype)
    for copy in later:
        copy.wait()


def early_first(own_set, other_set, drift_sets, diffusion_sets, block, speed, reward, other, out, *refs, half):
    keeps, (speed_rows, reward_rows), fields = refs[:2], refs[2:4], refs[4:]
    place = where_am_i()
    for field in fields:
        clear_pads(field, speed.shape[1])
    lay_rows(place, speed, reward, other, speed_rows, reward_rows)
    sets = own_set, other_set, drift_sets, diffusion_sets
    early_march(place, sets, half, block, speed_rows, reward_rows, out, keeps, fields)


def rest_first(own_set, other_set, drift_sets, diffusion_sets, first, speed_rows, reward_rows, edge, *refs, half):
    edge_other, keeps, out, fields, block, lower_rows = refs[0], refs[1:3], refs[3], refs[4:6], refs[6], refs[7]
    place = where_am_i()
    ny = speed_rows.shape[1]
    for field in (block, *fields):
        clear_pads(field, ny)
    for row in range(SUBSTEPS):
        block[SUBSTEPS - 1 - row, pl.ds(PAD, ny), :] = edge[row].astype(jnp.float32)
    for row in range(2):
        block[SUBSTEPS + row] = first[row]
    lay_lower(edge, edge_other, lower_rows)
    sets = own_set, other_set, drift_sets, diffusion_sets
    rest_march(place, sets, edge, lower_rows, block, speed_rows, reward_rows, out, keeps, fields)


def early_later(own_set, other_set, drift_sets, diffusion_sets, current, across, speed_rows, reward_rows, out, *refs, half):
    keeps, fields, block = refs[:2], refs[2:4], refs[4]
    place = where_am_i()
    for field in (block, *fields):
        clear_pads(field, speed_rows.shape[1])
    for q in range(half):
        spread(place, current, q, block, q)
    for row in range(SUBSTEPS):
        spread(place, across, SUBSTEPS - 1 - row, block, half + row)
    early_march(place, (own_set, other_set, drift_sets, diffusion_sets), half, block, speed_rows, reward_rows, out, keeps, fields)


def rest_later(own_set, other_set, drift_sets, diffusion_sets, current, beyond, speed_rows, reward_rows, edge, *refs, half):
    edge_other, keeps, out, fields, block, lower_rows = refs[0], refs[1:3], refs[3], refs[4:6], refs[6], refs[7]
    place = where_am_i()
    for field in (block, *fields):
        clear_pads(field, speed_rows.shape[1])
    for row in range(SUBSTEPS):
        spread(place, beyond, row, block, SUBSTEPS - 1 - row)
    for row in range(2):
        spread(place, current, row, block, SUBSTEPS + row)
    lay_lower(edge, edge_other, lower_rows)
    sets = own_set, other_set, drift_sets, diffusion_sets
    rest_march(place, sets, edge, lower_rows, block, speed_rows, reward_rows, out, keeps, fields)


def body(value, speed, reward, ctrl_set, drift_sets, diffusion_sets):
    own, cells, ny, nz = reward.shape
    count = 2 * own
    slabs, members = lax.axis_size("slab"), lax.axis_size("ctrl")
    chips, half = members // 2, cells // 2
    width = ny // chips
    chip, upper, _ = where_am_i()
    margin = SUBSTEPS - 1
    narrow, wire = jnp.bfloat16, jnp.float16
    both = ("slab", "ctrl")

    def device(s, z, c):
        return s * members + 2 * z + c

    partners = [(i, i ^ 1) for i in range(members)]

    facing, beside = [], []
    for s in range(slabs - 1):
        for z in range(chips):
            c = (s + 1) % 2
            facing += [(device(s, z, c), device(s + 1, z, c)), (device(s + 1, z, c), device(s, z, c))]
            beside += [(device(s, z, 1 - c), device(s + 1, z, c)), (device(s + 1, z, 1 - c), device(s, z, c))]

    whole = pl.BlockSpec(memory_space=pltpu.VMEM)
    scalars = pl.BlockSpec(memory_space=pltpu.SMEM)
    def shape(*dims):
        return jax.ShapeDtypeStruct(dims, jnp.float32)

    def call(kernel, rows, marched, arrays, outs):
        field = pltpu.VMEM((rows, ny + 2 * PAD, nz), jnp.float32)
        scratch = [field] * (2 if kernel is early_first else 3)
        if kernel in (rest_first, rest_later):
            scratch.append(pltpu.VMEM((count * margin, ny, nz), narrow))
        return pl.pallas_call(
            functools.partial(kernel, half=half),
            out_shape=outs,
            in_specs=[scalars] * 4 + [whole] * len(arrays),
            out_specs=jax.tree.map(lambda _: whole, outs),
            scratch_shapes=scratch,
            compiler_params=pltpu.CompilerParams(vmem_limit_bytes=32 * 2**20),
            cost_estimate=pl.CostEstimate(
                flops=25 * count * marched * ny * nz, bytes_accessed=12 * count * marched * ny * nz, transcendentals=0
            ),
        )(ctrl_set, other_set, drift_sets, diffusion_sets, *arrays)

    keeps = [shape(count, 2, ny, nz)] * (SUBSTEPS - 1)

    rows, given = half + SUBSTEPS, half + margin
    other_set = lax.ppermute(ctrl_set, "ctrl", partners)
    other = lax.ppermute(reward, "ctrl", partners)
    anywhere = pl.BlockSpec(memory_space=pl.ANY)
    dma = pltpu.SemaphoreType.DMA
    packed, far, block = pl.pallas_call(
        pack_kernel,
        out_shape=[
            pltpu.VMEM((SUBSTEPS + margin + own * margin, ny, nz), narrow),
            pltpu.VMEM((own * margin, ny, nz), narrow),
            pltpu.VMEM((rows, ny + 2 * PAD, nz), jnp.float32),
        ],
        in_specs=[anywhere] * 3,
        out_specs=[whole] * 3,
        scratch_shapes=[
            pltpu.VMEM((margin, ny, nz), jnp.float32),
            dma((rows,)),
            dma((margin,)),
            dma((own * margin,)),
            dma((own * margin,)),
        ],
    )(value, speed, reward)
    packed, far, other_set = lax.optimization_barrier((packed, far, other_set))
    edge = lax.ppermute(packed, both, facing)
    edge_other = lax.ppermute(far, both, beside)

    def reduce(best):
        parts = best.astype(wire)
        mine = parts[0]
        for step in range(chips - 1, 0, -1):
            pairs = [(2 * z + c, 2 * mate(z, step, chips) + c) for z in range(chips) for c in range(2)]
            mine = jnp.maximum(mine, lax.ppermute(parts[step], "ctrl", pairs))
        return mine

    def gather(mine):
        pieces = []
        for step in range(chips - 1, 0, -1):
            pairs = [(2 * mate(z, step, chips) + c, 2 * z + c) for z in range(chips) for c in range(2)]
            pieces.append(lax.ppermute(mine, "ctrl", pairs))
        return jnp.stack([mine, *pieces[::-1]])

    steps = sum(half + SUBSTEPS - 2 - 2 * k for k in range(SUBSTEPS))
    early_out = [shape(chips, half - SUBSTEPS, width, nz)] + keeps
    rest_out = shape(chips, SUBSTEPS, width, nz)
    rest_rows, rest_steps = 2 * SUBSTEPS + 2, SUBSTEPS * SUBSTEPS

    best, keep_a, keep_b, speed_rows, reward_rows = call(
        early_first,
        rows,
        steps,
        (block, speed, reward, other),
        early_out + [shape(given, ny, nz), shape(count, given, ny, nz)],
    )
    laid, edges = (speed_rows, reward_rows), (edge, edge_other)
    best_rest = call(rest_first, rest_rows, rest_steps, (block, *laid, *edges, keep_a, keep_b), rest_out)
    pieces = gather(reduce(jnp.concatenate([best_rest, best], axis=1)))

    across = lax.ppermute(pieces[:, -SUBSTEPS:], "ctrl", partners)
    beyond = lax.ppermute(pieces[:, :SUBSTEPS].astype(narrow), both, facing)
    current = pieces.astype(jnp.float32)
    best, *kept = call(early_later, rows, steps, (current, across.astype(jnp.float32), *laid), early_out)
    best_rest = call(
        rest_later, rest_rows, rest_steps, (current, beyond, *laid, *edges, *kept), rest_out
    )
    pieces = gather(reduce(jnp.concatenate([best_rest, best], axis=1)))

    from_partner = lax.ppermute(pieces, "ctrl", partners)
    low_half = jnp.where(upper == 0, pieces, from_partner)
    high_half = jnp.where(upper == 0, from_partner, pieces)[:, ::-1]
    slab_pieces = jnp.concatenate([low_half, high_half], axis=1)
    ordered = [
        lax.dynamic_index_in_dim(slab_pieces, mate_step(chip, shard, chips), 0, keepdims=False)
        for shard in range(chips)
    ]
    return jnp.concatenate(ordered, axis=1).astype(jnp.float32)


def solution(mesh):
    in_specs = (
        P("slab", None, None),
        P("slab", None, None),
        P("ctrl", "slab", None, None),
        P("ctrl"),
        P(),
        P(),
    )
    out_specs = P("slab", None, None)
    return jax.shard_map(body, mesh=mesh, in_specs=in_specs, out_specs=out_specs, check_vma=False)
```

```python
import functools

import jax
import jax.numpy as jnp
from jax import lax
from jax.experimental import pallas as pl
from jax.experimental.pallas import tpu as pltpu
from jax.sharding import PartitionSpec as P

SUBSTEPS = 3
PAD = 8
CHUNK = 32
LOWEST = -3.0e38


def mate(chip, step, chips):
    if chips & (chips - 1) == 0:
        return chip ^ step
    return (chip + step) % chips


def mate_step(chip, other, chips):
    if chips & (chips - 1) == 0:
        return chip ^ other
    return (other - chip) % chips


def where_am_i():
    slab, member = lax.axis_index("slab"), lax.axis_index("ctrl")
    upper = (member + slab) % 2
    end = jnp.where(upper == 0, 0, lax.axis_size("slab") - 1)
    return member // 2, upper, jnp.where(slab == end, 0, 1)


def coefficients(sets, ctrl):
    own_set, other_set, drift_sets, diffusion_sets = sets
    own = own_set.shape[0]
    kind = jnp.where(ctrl < own, own_set[jnp.minimum(ctrl, own - 1)], other_set[jnp.maximum(ctrl - own, 0)])
    rates = [diffusion_sets[kind, dim] for dim in range(3)]
    drifts = [drift_sets[kind, dim] for dim in range(3)]
    sizes = [jnp.maximum(drift, -drift) for drift in drifts]
    return rates, sizes, 1.0 - 2.0 * (rates[0] + rates[1] + rates[2]), sizes[0] + sizes[1] + sizes[2], drifts


def taps(src, rows, first, size):
    lines = pl.ds(PAD + first, size)
    behind, center = src[rows[0] - 1, lines, :], src[rows[0], lines, :]
    nz = center.shape[1]
    lane = lax.broadcasted_iota(jnp.int32, center.shape, 1)
    for row in rows:
        ahead = src[row + 1, lines, :]
        y_ahead = src[row, pl.ds(PAD + first + 1, size), :]
        y_behind = src[row, pl.ds(PAD + first - 1, size), :]
        z_ahead = jnp.where(lane == nz - 1, 0.0, pltpu.roll(center, nz - 1, 1))
        z_behind = jnp.where(lane == 0, 0.0, pltpu.roll(center, 1, 1))
        yield row, center, ((ahead, behind), (y_ahead, y_behind), (z_ahead, z_behind))
        behind, center = center, ahead


def blend(coef, ups, center, sides, sums, speed, reward):
    rates, sizes, weight, size, _ = coef
    winds = [jnp.where(up, *side) for up, side in zip(ups, sides)]
    still = reward + weight * center + rates[0] * sums[0]
    still = still + rates[1] * sums[1] + rates[2] * sums[2]
    wind = sizes[0] * winds[0] + sizes[1] * winds[1] + sizes[2] * winds[2]
    return still + speed * (wind - size * center)


def sweep(place, sets, ctrls, src, rows, speed, reward, store):
    ny = src.shape[1] - 2 * PAD
    coefs = [coefficients(sets, ctrl) for ctrl in ctrls]
    ups = [winds_of(place, coef[4]) for coef in coefs]
    size = min(ny, CHUNK)
    for first in range(0, ny, size):
        spot = pl.ds(first, size)
        for row, center, sides in taps(src, rows, first, size):
            sums = [ahead + behind for ahead, behind in sides]
            pace = speed(row, spot)
            for ctrl, coef, up in zip(ctrls, coefs, ups):
                store(ctrl, row, first, size, blend(coef, up, center, sides, sums, pace, reward(ctrl, row, spot)))


def winds_of(place, drifts):
    x_up = jnp.where(place[1] == 0, drifts[0], -drifts[0]) > 0.0
    return x_up, drifts[1] > 0.0, drifts[2] > 0.0


def put_max(place, out, index, first, new):
    chips, width = out.shape[0], out.shape[2]
    size = min(width, new.shape[0])
    for part in range(0, new.shape[0], size):
        spot = mate_step(place[0], (first + part) // width, chips)
        lines = pl.ds((first + part) % width, size)
        out[spot, index, lines, :] = jnp.maximum(out[spot, index, lines, :], new[part : part + size])


def start_max(out):
    for shard in range(out.shape[0]):
        for row in range(out.shape[1]):
            out[shard, row] = jnp.full(out.shape[2:], LOWEST, out.dtype)


def clear_pads(field, ny):
    if len(field.shape) > 3:
        for part in range(field.shape[0]):
            clear_pads(field.at[part], ny)
        return
    zero = jnp.zeros((PAD, field.shape[2]), field.dtype)
    for row in range(field.shape[0]):
        field[row, 0:PAD, :] = zero
        field[row, PAD + ny : 2 * PAD + ny, :] = zero


def lay_rows(place, speed, reward, other, speed_rows, reward_rows):
    own, cells = reward.shape[:2]
    for q in range(speed_rows.shape[0]):
        real = jnp.where(place[1] == 0, q, cells - 1 - q)
        speed_rows[q] = speed[real]
        for ctrl in range(own):
            reward_rows[ctrl, q] = reward[ctrl, real].astype(jnp.float32)
            reward_rows[own + ctrl, q] = other[ctrl, real].astype(jnp.float32)


def lay_lower(edge, edge_other, lower_rows):
    mine = edge_other.shape[0]
    for row in range(mine):
        lower_rows[row] = edge[edge.shape[0] - mine + row]
        lower_rows[mine + row] = edge_other[row]


def spread(place, pieces, index, field, row):
    chips, width = pieces.shape[0], pieces.shape[2]
    for shard in range(chips):
        piece = pieces[mate_step(place[0], shard, chips), index]
        field[row, pl.ds(PAD + shard * width, width), :] = piece.astype(field.dtype)


def early_march(place, sets, half, block, speed_rows, reward_rows, out, keeps, fields):
    count = reward_rows.shape[0]
    start_max(out)

    def speed(q, spot):
        return speed_rows[q, spot, :]

    def reward(ctrl, q, spot):
        return reward_rows[ctrl, q, spot, :]

    def keep(substep, ctrl, q, first, size, new):
        if q < substep + 3:
            keeps[substep][ctrl, q - substep - 1, pl.ds(first, size), :] = new

    def store(ctrl, q, first, size, new):
        fields[0][ctrl, q, pl.ds(PAD + first, size), :] = new
        keep(0, ctrl, q, first, size, new)

    sweep(place, sets, range(count), block, range(1, half + SUBSTEPS - 1), speed, reward, store)

    def one(ctrl, carry):
        source = fields[0].at[ctrl]
        for substep in range(1, SUBSTEPS):
            last = substep == SUBSTEPS - 1

            def store(ctrl, q, first, size, new, substep=substep, last=last):
                if last:
                    put_max(place, out, q - SUBSTEPS, first, new)
                    return
                fields[substep][q, pl.ds(PAD + first, size), :] = new
                keep(substep, ctrl, q, first, size, new)

            rows = range(1 + substep, half + SUBSTEPS - 1 - substep)
            sweep(place, sets, [ctrl], source, rows, speed, reward, store)
            source = None if last else fields[substep]
        return carry

    lax.fori_loop(0, count, one, 0)


def rest_march(place, sets, edge, lower_rows, block, speed_rows, reward_rows, out, keeps, fields):
    ny = block.shape[1] - 2 * PAD
    count = reward_rows.shape[0]
    margin = SUBSTEPS - 1
    inside = place[2].astype(jnp.float32)
    start_max(out)

    def speed(row, spot):
        q = row - SUBSTEPS
        if q < 0:
            return edge[SUBSTEPS - 1 - q, spot, :].astype(jnp.float32)
        return speed_rows[q, spot, :]

    def reward(ctrl, row, spot):
        q = row - SUBSTEPS
        if q < 0:
            return lower_rows[ctrl * margin - 1 - q, spot, :].astype(jnp.float32)
        return reward_rows[ctrl, q, spot, :]

    def store(ctrl, row, first, size, new):
        fields[0][ctrl, row, pl.ds(PAD + first, size), :] = new * inside if row < SUBSTEPS else new

    sweep(place, sets, range(count), block, range(1, SUBSTEPS + 1), speed, reward, store)

    def one(ctrl, carry):
        source = fields[0].at[ctrl]
        for substep in range(1, SUBSTEPS):
            last = substep == SUBSTEPS - 1
            for kept in range(2):
                source[substep + kept + SUBSTEPS, pl.ds(PAD, ny), :] = keeps[substep - 1][ctrl, kept]

            def store(ctrl, row, first, size, new, substep=substep, last=last):
                if last:
                    put_max(place, out, row - SUBSTEPS, first, new)
                    return
                new = new * inside if row < SUBSTEPS else new
                fields[substep][row, pl.ds(PAD + first, size), :] = new

            rows = range(1 + substep, SUBSTEPS + 1 + substep)
            sweep(place, sets, [ctrl], source, rows, speed, reward, store)
            source = None if last else fields[substep]
        return carry

    lax.fori_loop(0, count, one, 0)


def pack_kernel(value, speed, reward, edge, far, block, speed_rows, value_sem, speed_sem, near_sem, far_sem):
    place = where_am_i()
    cells, ny = value.shape[:2]
    own = reward.shape[0]
    margin = SUBSTEPS - 1
    copies, later = [], []
    for row in range(SUBSTEPS):
        near = jnp.where(place[1] == 0, row, cells - 1 - row)
        away = jnp.where(place[1] == 0, cells - 1 - row, row)
        copies.append(pltpu.make_async_copy(value.at[near], block.at[row, pl.ds(PAD, ny)], value_sem.at[row]))
        if row < margin:
            copies.append(pltpu.make_async_copy(speed.at[near], speed_rows.at[row], speed_sem.at[row]))
            for ctrl in range(own):
                spot = ctrl * margin + row
                place_near = edge.at[SUBSTEPS + margin + spot]
                later.append(pltpu.make_async_copy(reward.at[ctrl, near], place_near, near_sem.at[spot]))
                later.append(pltpu.make_async_copy(reward.at[ctrl, away], far.at[spot], far_sem.at[spot]))
    for row in range(SUBSTEPS, block.shape[0]):
        real = jnp.where(place[1] == 0, row, cells - 1 - row)
        later.append(pltpu.make_async_copy(value.at[real], block.at[row, pl.ds(PAD, ny)], value_sem.at[row]))
    for copy in copies + later:
        copy.start()
    clear_pads(block, ny)
    for copy in copies:
        copy.wait()
    for row in range(SUBSTEPS):
        edge[row] = block[row, pl.ds(PAD, ny), :].astype(edge.dtype)
    for row in range(margin):
        edge[SUBSTEPS + row] = speed_rows[row].astype(edge.dtype)
    for copy in later:
        copy.wait()


def early_first(own_set, other_set, drift_sets, diffusion_sets, block, speed, reward, other, out, *refs, half):
    keeps, (speed_rows, reward_rows), fields = refs[:2], refs[2:4], refs[4:]
    place = where_am_i()
    for field in fields:
        clear_pads(field, speed.shape[1])
    lay_rows(place, speed, reward, other, speed_rows, reward_rows)
    sets = own_set, other_set, drift_sets, diffusion_sets
    early_march(place, sets, half, block, speed_rows, reward_rows, out, keeps, fields)


def rest_first(own_set, other_set, drift_sets, diffusion_sets, first, speed_rows, reward_rows, edge, *refs, half):
    edge_other, keeps, out, fields, block, lower_rows = refs[0], refs[1:3], refs[3], refs[4:6], refs[6], refs[7]
    place = where_am_i()
    ny = speed_rows.shape[1]
    for field in (block, *fields):
        clear_pads(field, ny)
    for row in range(SUBSTEPS):
        block[SUBSTEPS - 1 - row, pl.ds(PAD, ny), :] = edge[row].astype(jnp.float32)
    for row in range(2):
        block[SUBSTEPS + row] = first[row]
    lay_lower(edge, edge_other, lower_rows)
    sets = own_set, other_set, drift_sets, diffusion_sets
    rest_march(place, sets, edge, lower_rows, block, speed_rows, reward_rows, out, keeps, fields)


def early_later(own_set, other_set, drift_sets, diffusion_sets, current, across, speed_rows, reward_rows, out, *refs, half):
    keeps, fields, block = refs[:2], refs[2:4], refs[4]
    place = where_am_i()
    for field in (block, *fields):
        clear_pads(field, speed_rows.shape[1])
    for q in range(half):
        spread(place, current, q, block, q)
    for row in range(SUBSTEPS):
        spread(place, across, SUBSTEPS - 1 - row, block, half + row)
    early_march(place, (own_set, other_set, drift_sets, diffusion_sets), half, block, speed_rows, reward_rows, out, keeps, fields)


def rest_later(own_set, other_set, drift_sets, diffusion_sets, current, beyond, speed_rows, reward_rows, edge, *refs, half):
    edge_other, keeps, out, fields, block, lower_rows = refs[0], refs[1:3], refs[3], refs[4:6], refs[6], refs[7]
    place = where_am_i()
    for field in (block, *fields):
        clear_pads(field, speed_rows.shape[1])
    for row in range(SUBSTEPS):
        spread(place, beyond, row, block, SUBSTEPS - 1 - row)
    for row in range(2):
        spread(place, current, row, block, SUBSTEPS + row)
    lay_lower(edge, edge_other, lower_rows)
    sets = own_set, other_set, drift_sets, diffusion_sets
    rest_march(place, sets, edge, lower_rows, block, speed_rows, reward_rows, out, keeps, fields)


def body(value, speed, reward, ctrl_set, drift_sets, diffusion_sets):
    own, cells, ny, nz = reward.shape
    count = 2 * own
    slabs, members = lax.axis_size("slab"), lax.axis_size("ctrl")
    chips, half = members // 2, cells // 2
    width = ny // chips
    chip, upper, _ = where_am_i()
    margin = SUBSTEPS - 1
    narrow, wire = jnp.bfloat16, jnp.float16
    both = ("slab", "ctrl")

    def device(s, z, c):
        return s * members + 2 * z + c

    partners = [(i, i ^ 1) for i in range(members)]

    facing, beside = [], []
    for s in range(slabs - 1):
        for z in range(chips):
            c = (s + 1) % 2
            facing += [(device(s, z, c), device(s + 1, z, c)), (device(s + 1, z, c), device(s, z, c))]
            beside += [(device(s, z, 1 - c), device(s + 1, z, c)), (device(s + 1, z, 1 - c), device(s, z, c))]

    whole = pl.BlockSpec(memory_space=pltpu.VMEM)
    scalars = pl.BlockSpec(memory_space=pltpu.SMEM)
    def shape(*dims):
        return jax.ShapeDtypeStruct(dims, jnp.float32)

    def call(kernel, rows, marched, arrays, outs):
        field = pltpu.VMEM((rows, ny + 2 * PAD, nz), jnp.float32)
        scratch = [pltpu.VMEM((count, rows, ny + 2 * PAD, nz), jnp.float32)] + [field] * (SUBSTEPS - 2)
        if kernel is not early_first:
            scratch.append(field)
        if kernel in (rest_first, rest_later):
            scratch.append(pltpu.VMEM((count * margin, ny, nz), narrow))
        return pl.pallas_call(
            functools.partial(kernel, half=half),
            out_shape=outs,
            in_specs=[scalars] * 4 + [whole] * len(arrays),
            out_specs=jax.tree.map(lambda _: whole, outs),
            scratch_shapes=scratch,
            compiler_params=pltpu.CompilerParams(vmem_limit_bytes=16 * 2**20),
            cost_estimate=pl.CostEstimate(
                flops=25 * count * marched * ny * nz, bytes_accessed=12 * count * marched * ny * nz, transcendentals=0
            ),
        )(ctrl_set, other_set, drift_sets, diffusion_sets, *arrays)

    keeps = [shape(count, 2, ny, nz)] * (SUBSTEPS - 1)

    rows, given = half + SUBSTEPS, half + margin
    other_set = lax.ppermute(ctrl_set, "ctrl", partners)
    other = lax.ppermute(reward, "ctrl", partners)
    anywhere = pl.BlockSpec(memory_space=pl.ANY)
    dma = pltpu.SemaphoreType.DMA
    packed, far, block = pl.pallas_call(
        pack_kernel,
        out_shape=[
            pltpu.VMEM((SUBSTEPS + margin + own * margin, ny, nz), narrow),
            pltpu.VMEM((own * margin, ny, nz), narrow),
            pltpu.VMEM((rows, ny + 2 * PAD, nz), jnp.float32),
        ],
        in_specs=[anywhere] * 3,
        out_specs=[whole] * 3,
        scratch_shapes=[
            pltpu.VMEM((margin, ny, nz), jnp.float32),
            dma((rows,)),
            dma((margin,)),
            dma((own * margin,)),
            dma((own * margin,)),
        ],
    )(value, speed, reward)
    packed, far, other_set = lax.optimization_barrier((packed, far, other_set))
    edge = lax.ppermute(packed, both, facing)
    edge_other = lax.ppermute(far, both, beside)

    def reduce(best):
        parts = best.astype(wire)
        mine = parts[0]
        for step in range(chips - 1, 0, -1):
            pairs = [(2 * z + c, 2 * mate(z, step, chips) + c) for z in range(chips) for c in range(2)]
            mine = jnp.maximum(mine, lax.ppermute(parts[step], "ctrl", pairs))
        return mine

    def gather(mine):
        pieces = []
        for step in range(chips - 1, 0, -1):
            pairs = [(2 * mate(z, step, chips) + c, 2 * z + c) for z in range(chips) for c in range(2)]
            pieces.append(lax.ppermute(mine, "ctrl", pairs))
        return jnp.stack([mine, *pieces[::-1]])

    steps = sum(half + SUBSTEPS - 2 - 2 * k for k in range(SUBSTEPS))
    early_out = [shape(chips, half - SUBSTEPS, width, nz)] + keeps
    rest_out = shape(chips, SUBSTEPS, width, nz)
    rest_rows, rest_steps = 2 * SUBSTEPS + 2, SUBSTEPS * SUBSTEPS

    best, keep_a, keep_b, speed_rows, reward_rows = call(
        early_first,
        rows,
        steps,
        (block, speed, reward, other),
        early_out + [shape(given, ny, nz), shape(count, given, ny, nz)],
    )
    laid, edges = (speed_rows, reward_rows), (edge, edge_other)
    best_rest = call(rest_first, rest_rows, rest_steps, (block, *laid, *edges, keep_a, keep_b), rest_out)
    pieces = gather(reduce(jnp.concatenate([best_rest, best], axis=1)))

    across = lax.ppermute(pieces[:, -SUBSTEPS:], "ctrl", partners)
    beyond = lax.ppermute(pieces[:, :SUBSTEPS].astype(narrow), both, facing)
    current = pieces.astype(jnp.float32)
    best, *kept = call(early_later, rows, steps, (current, across.astype(jnp.float32), *laid), early_out)
    best_rest = call(
        rest_later, rest_rows, rest_steps, (current, beyond, *laid, *edges, *kept), rest_out
    )
    pieces = gather(reduce(jnp.concatenate([best_rest, best], axis=1)))

    from_partner = lax.ppermute(pieces, "ctrl", partners)
    low_half = jnp.where(upper == 0, pieces, from_partner)
    high_half = jnp.where(upper == 0, from_partner, pieces)[:, ::-1]
    slab_pieces = jnp.concatenate([low_half, high_half], axis=1)
    ordered = [
        lax.dynamic_index_in_dim(slab_pieces, mate_step(chip, shard, chips), 0, keepdims=False)
        for shard in range(chips)
    ]
    return jnp.concatenate(ordered, axis=1).astype(jnp.float32)


def solution(mesh):
    in_specs = (
        P("slab", None, None),
        P("slab", None, None),
        P("ctrl", "slab", None, None),
        P("ctrl"),
        P(),
        P(),
    )
    out_specs = P("slab", None, None)
    return jax.shard_map(body, mesh=mesh, in_specs=in_specs, out_specs=out_specs, check_vma=False)
```

```python
import functools

import jax
import jax.numpy as jnp
from jax import lax
from jax.experimental import pallas as pl
from jax.experimental.pallas import tpu as pltpu
from jax.sharding import PartitionSpec as P

SUBSTEPS = 3
PAD = 8
CHUNK = 32
LOWEST = -3.0e38


def mate(chip, step, chips):
    if chips & (chips - 1) == 0:
        return chip ^ step
    return (chip + step) % chips


def mate_step(chip, other, chips):
    if chips & (chips - 1) == 0:
        return chip ^ other
    return (other - chip) % chips


def where_am_i():
    slab, member = lax.axis_index("slab"), lax.axis_index("ctrl")
    upper = (member + slab) % 2
    end = jnp.where(upper == 0, 0, lax.axis_size("slab") - 1)
    return member // 2, upper, jnp.where(slab == end, 0, 1)


def coefficients(coef, ctrl):
    rates = [coef[ctrl, dim] for dim in range(3)]
    drifts = [coef[ctrl, 3 + dim] for dim in range(3)]
    sizes = [jnp.maximum(drift, -drift) for drift in drifts]
    return rates, sizes, 1.0 - 2.0 * (rates[0] + rates[1] + rates[2]), sizes[0] + sizes[1] + sizes[2], drifts


def taps(src, rows, first, size):
    lines = pl.ds(PAD + first, size)
    behind, center = src[rows[0] - 1, lines, :], src[rows[0], lines, :]
    nz = center.shape[1]
    lane = lax.broadcasted_iota(jnp.int32, center.shape, 1)
    for row in rows:
        ahead = src[row + 1, lines, :]
        y_ahead = src[row, pl.ds(PAD + first + 1, size), :]
        y_behind = src[row, pl.ds(PAD + first - 1, size), :]
        z_ahead = jnp.where(lane == nz - 1, 0.0, pltpu.roll(center, nz - 1, 1))
        z_behind = jnp.where(lane == 0, 0.0, pltpu.roll(center, 1, 1))
        yield row, center, ((ahead, behind), (y_ahead, y_behind), (z_ahead, z_behind))
        behind, center = center, ahead


def blend(coef, ups, center, sides, sums, speed, reward):
    rates, sizes, weight, size, _ = coef
    winds = [jnp.where(up, *side) for up, side in zip(ups, sides)]
    still = reward + weight * center + rates[0] * sums[0]
    still = still + rates[1] * sums[1] + rates[2] * sums[2]
    wind = sizes[0] * winds[0] + sizes[1] * winds[1] + sizes[2] * winds[2]
    return still + speed * (wind - size * center)


def sweep(place, coef, ctrls, src, rows, speed, reward, store):
    ny = src.shape[1] - 2 * PAD
    coefs = [coefficients(coef, ctrl) for ctrl in ctrls]
    ups = [winds_of(place, own_coef[4]) for own_coef in coefs]
    size = min(ny, CHUNK)
    for first in range(0, ny, size):
        spot = pl.ds(first, size)
        for row, center, sides in taps(src, rows, first, size):
            sums = [ahead + behind for ahead, behind in sides]
            pace = speed(row, spot)
            for ctrl, own_coef, up in zip(ctrls, coefs, ups):
                store(ctrl, row, first, size, blend(own_coef, up, center, sides, sums, pace, reward(ctrl, row, spot)))


def winds_of(place, drifts):
    x_up = jnp.where(place[1] == 0, drifts[0], -drifts[0]) > 0.0
    return x_up, drifts[1] > 0.0, drifts[2] > 0.0


def put_max(place, out, index, first, new):
    chips, width = out.shape[0], out.shape[2]
    size = min(width, new.shape[0])
    for part in range(0, new.shape[0], size):
        spot = mate_step(place[0], (first + part) // width, chips)
        lines = pl.ds((first + part) % width, size)
        out[spot, index, lines, :] = jnp.maximum(out[spot, index, lines, :], new[part : part + size])


def start_max(out):
    for shard in range(out.shape[0]):
        for row in range(out.shape[1]):
            out[shard, row] = jnp.full(out.shape[2:], LOWEST, out.dtype)


def clear_pads(field, ny):
    if len(field.shape) > 3:
        for part in range(field.shape[0]):
            clear_pads(field.at[part], ny)
        return
    zero = jnp.zeros((PAD, field.shape[2]), field.dtype)
    for row in range(field.shape[0]):
        field[row, 0:PAD, :] = zero
        field[row, PAD + ny : 2 * PAD + ny, :] = zero


def lay_rows(place, speed, reward, other, speed_rows, reward_rows):
    own, cells = reward.shape[:2]
    for q in range(speed_rows.shape[0]):
        real = jnp.where(place[1] == 0, q, cells - 1 - q)
        speed_rows[q] = speed[real]
        for ctrl in range(own):
            reward_rows[ctrl, q] = reward[ctrl, real].astype(jnp.float32)
            reward_rows[own + ctrl, q] = other[ctrl, real].astype(jnp.float32)


def lay_lower(edge, edge_other, lower_rows):
    mine = edge_other.shape[0]
    for row in range(mine):
        lower_rows[row] = edge[edge.shape[0] - mine + row]
        lower_rows[mine + row] = edge_other[row]


def spread(place, pieces, index, field, row):
    chips, width = pieces.shape[0], pieces.shape[2]
    for shard in range(chips):
        piece = pieces[mate_step(place[0], shard, chips), index]
        field[row, pl.ds(PAD + shard * width, width), :] = piece.astype(field.dtype)


def early_march(place, coef, half, block, speed_rows, reward_rows, out, keeps, fields):
    count = reward_rows.shape[0]
    start_max(out)

    def speed(q, spot):
        return speed_rows[q, spot, :]

    def reward(ctrl, q, spot):
        return reward_rows[ctrl, q, spot, :]

    def keep(substep, ctrl, q, first, size, new):
        if q < substep + 3:
            keeps[substep][ctrl, q - substep - 1, pl.ds(first, size), :] = new

    def store(ctrl, q, first, size, new):
        fields[0][ctrl, q, pl.ds(PAD + first, size), :] = new
        keep(0, ctrl, q, first, size, new)

    sweep(place, coef, range(count), block, range(1, half + SUBSTEPS - 1), speed, reward, store)

    def one(ctrl, carry):
        source = fields[0].at[ctrl]
        for substep in range(1, SUBSTEPS):
            last = substep == SUBSTEPS - 1

            def store(ctrl, q, first, size, new, substep=substep, last=last):
                if last:
                    put_max(place, out, q - SUBSTEPS, first, new)
                    return
                fields[substep][q, pl.ds(PAD + first, size), :] = new
                keep(substep, ctrl, q, first, size, new)

            rows = range(1 + substep, half + SUBSTEPS - 1 - substep)
            sweep(place, coef, [ctrl], source, rows, speed, reward, store)
            source = None if last else fields[substep]
        return carry

    lax.fori_loop(0, count, one, 0)


def rest_march(place, coef, edge, lower_rows, block, speed_rows, reward_rows, out, keeps, fields):
    ny = block.shape[1] - 2 * PAD
    count = reward_rows.shape[0]
    margin = SUBSTEPS - 1
    inside = place[2].astype(jnp.float32)
    start_max(out)

    def speed(row, spot):
        q = row - SUBSTEPS
        if q < 0:
            return edge[SUBSTEPS - 1 - q, spot, :].astype(jnp.float32)
        return speed_rows[q, spot, :]

    def reward(ctrl, row, spot):
        q = row - SUBSTEPS
        if q < 0:
            return lower_rows[ctrl * margin - 1 - q, spot, :].astype(jnp.float32)
        return reward_rows[ctrl, q, spot, :]

    def store(ctrl, row, first, size, new):
        fields[0][ctrl, row, pl.ds(PAD + first, size), :] = new * inside if row < SUBSTEPS else new

    sweep(place, coef, range(count), block, range(1, SUBSTEPS + 1), speed, reward, store)

    def one(ctrl, carry):
        source = fields[0].at[ctrl]
        for substep in range(1, SUBSTEPS):
            last = substep == SUBSTEPS - 1
            for kept in range(2):
                source[substep + kept + SUBSTEPS, pl.ds(PAD, ny), :] = keeps[substep - 1][ctrl, kept]

            def store(ctrl, row, first, size, new, substep=substep, last=last):
                if last:
                    put_max(place, out, row - SUBSTEPS, first, new)
                    return
                new = new * inside if row < SUBSTEPS else new
                fields[substep][row, pl.ds(PAD + first, size), :] = new

            rows = range(1 + substep, SUBSTEPS + 1 + substep)
            sweep(place, coef, [ctrl], source, rows, speed, reward, store)
            source = None if last else fields[substep]
        return carry

    lax.fori_loop(0, count, one, 0)


def pack_kernel(value, speed, reward, edge, far, block, speed_rows, value_sem, speed_sem, near_sem, far_sem):
    place = where_am_i()
    cells, ny = value.shape[:2]
    own = reward.shape[0]
    margin = SUBSTEPS - 1
    copies, later = [], []
    for row in range(SUBSTEPS):
        near = jnp.where(place[1] == 0, row, cells - 1 - row)
        away = jnp.where(place[1] == 0, cells - 1 - row, row)
        copies.append(pltpu.make_async_copy(value.at[near], block.at[row, pl.ds(PAD, ny)], value_sem.at[row]))
        if row < margin:
            copies.append(pltpu.make_async_copy(speed.at[near], speed_rows.at[row], speed_sem.at[row]))
            for ctrl in range(own):
                spot = ctrl * margin + row
                place_near = edge.at[SUBSTEPS + margin + spot]
                later.append(pltpu.make_async_copy(reward.at[ctrl, near], place_near, near_sem.at[spot]))
                later.append(pltpu.make_async_copy(reward.at[ctrl, away], far.at[spot], far_sem.at[spot]))
    for row in range(SUBSTEPS, block.shape[0]):
        real = jnp.where(place[1] == 0, row, cells - 1 - row)
        later.append(pltpu.make_async_copy(value.at[real], block.at[row, pl.ds(PAD, ny)], value_sem.at[row]))
    for copy in copies + later:
        copy.start()
    clear_pads(block, ny)
    for copy in copies:
        copy.wait()
    for row in range(SUBSTEPS):
        edge[row] = block[row, pl.ds(PAD, ny), :].astype(edge.dtype)
    for row in range(margin):
        edge[SUBSTEPS + row] = speed_rows[row].astype(edge.dtype)
    for copy in later:
        copy.wait()


def early_first(coef, block, speed, reward, other, out, *refs, half):
    keeps, (speed_rows, reward_rows), fields = refs[:2], refs[2:4], refs[4:]
    place = where_am_i()
    for field in fields:
        clear_pads(field, speed.shape[1])
    lay_rows(place, speed, reward, other, speed_rows, reward_rows)
    early_march(place, coef, half, block, speed_rows, reward_rows, out, keeps, fields)


def rest_first(coef, first, speed_rows, reward_rows, edge, *refs, half):
    edge_other, keeps, out, fields, block, lower_rows = refs[0], refs[1:3], refs[3], refs[4:6], refs[6], refs[7]
    place = where_am_i()
    ny = speed_rows.shape[1]
    for field in (block, *fields):
        clear_pads(field, ny)
    for row in range(SUBSTEPS):
        block[SUBSTEPS - 1 - row, pl.ds(PAD, ny), :] = edge[row].astype(jnp.float32)
    for row in range(2):
        block[SUBSTEPS + row] = first[row]
    lay_lower(edge, edge_other, lower_rows)
    rest_march(place, coef, edge, lower_rows, block, speed_rows, reward_rows, out, keeps, fields)


def early_later(coef, current, across, speed_rows, reward_rows, out, *refs, half):
    keeps, fields, block = refs[:2], refs[2:4], refs[4]
    place = where_am_i()
    for field in (block, *fields):
        clear_pads(field, speed_rows.shape[1])
    for q in range(half):
        spread(place, current, q, block, q)
    for row in range(SUBSTEPS):
        spread(place, across, SUBSTEPS - 1 - row, block, half + row)
    early_march(place, coef, half, block, speed_rows, reward_rows, out, keeps, fields)


def rest_later(coef, current, beyond, speed_rows, reward_rows, edge, *refs, half):
    edge_other, keeps, out, fields, block, lower_rows = refs[0], refs[1:3], refs[3], refs[4:6], refs[6], refs[7]
    place = where_am_i()
    for field in (block, *fields):
        clear_pads(field, speed_rows.shape[1])
    for row in range(SUBSTEPS):
        spread(place, beyond, row, block, SUBSTEPS - 1 - row)
    for row in range(2):
        spread(place, current, row, block, SUBSTEPS + row)
    lay_lower(edge, edge_other, lower_rows)
    rest_march(place, coef, edge, lower_rows, block, speed_rows, reward_rows, out, keeps, fields)


def body(value, speed, reward, ctrl_set, drift_sets, diffusion_sets):
    own, cells, ny, nz = reward.shape
    count = 2 * own
    slabs, members = lax.axis_size("slab"), lax.axis_size("ctrl")
    chips, half = members // 2, cells // 2
    width = ny // chips
    chip, upper, _ = where_am_i()
    margin = SUBSTEPS - 1
    narrow, wire = jnp.bfloat16, jnp.float16
    both = ("slab", "ctrl")

    def device(s, z, c):
        return s * members + 2 * z + c

    partners = [(i, i ^ 1) for i in range(members)]

    facing, beside = [], []
    for s in range(slabs - 1):
        for z in range(chips):
            c = (s + 1) % 2
            facing += [(device(s, z, c), device(s + 1, z, c)), (device(s + 1, z, c), device(s, z, c))]
            beside += [(device(s, z, 1 - c), device(s + 1, z, c)), (device(s + 1, z, 1 - c), device(s, z, c))]

    whole = pl.BlockSpec(memory_space=pltpu.VMEM)
    scalars = pl.BlockSpec(memory_space=pltpu.SMEM)
    def shape(*dims):
        return jax.ShapeDtypeStruct(dims, jnp.float32)

    def call(kernel, rows, marched, arrays, outs):
        field = pltpu.VMEM((rows, ny + 2 * PAD, nz), jnp.float32)
        scratch = [pltpu.VMEM((count, rows, ny + 2 * PAD, nz), jnp.float32)] + [field] * (SUBSTEPS - 2)
        if kernel is not early_first:
            scratch.append(field)
        if kernel in (rest_first, rest_later):
            scratch.append(pltpu.VMEM((count * margin, ny, nz), narrow))
        return pl.pallas_call(
            functools.partial(kernel, half=half),
            out_shape=outs,
            in_specs=[scalars] + [whole] * len(arrays),
            out_specs=jax.tree.map(lambda _: whole, outs),
            scratch_shapes=scratch,
            compiler_params=pltpu.CompilerParams(vmem_limit_bytes=16 * 2**20),
            cost_estimate=pl.CostEstimate(
                flops=25 * count * marched * ny * nz, bytes_accessed=12 * count * marched * ny * nz, transcendentals=0
            ),
        )(coef, *arrays)

    keeps = [shape(count, 2, ny, nz)] * (SUBSTEPS - 1)

    rows, given = half + SUBSTEPS, half + margin
    other_set = lax.ppermute(ctrl_set, "ctrl", partners)
    other = lax.ppermute(reward, "ctrl", partners)
    anywhere = pl.BlockSpec(memory_space=pl.ANY)
    dma = pltpu.SemaphoreType.DMA
    packed, far, block = pl.pallas_call(
        pack_kernel,
        out_shape=[
            pltpu.VMEM((SUBSTEPS + margin + own * margin, ny, nz), narrow),
            pltpu.VMEM((own * margin, ny, nz), narrow),
            pltpu.VMEM((rows, ny + 2 * PAD, nz), jnp.float32),
        ],
        in_specs=[anywhere] * 3,
        out_specs=[whole] * 3,
        scratch_shapes=[
            pltpu.VMEM((margin, ny, nz), jnp.float32),
            dma((rows,)),
            dma((margin,)),
            dma((own * margin,)),
            dma((own * margin,)),
        ],
    )(value, speed, reward)
    packed, far, other_set = lax.optimization_barrier((packed, far, other_set))
    edge = lax.ppermute(packed, both, facing)
    edge_other = lax.ppermute(far, both, beside)

    sets = jnp.concatenate([ctrl_set, other_set])
    picked = sets[:, None] == jnp.arange(drift_sets.shape[0], dtype=jnp.int32)[None, :]
    pairs = jnp.concatenate([diffusion_sets, drift_sets], axis=1)
    coef = jnp.sum(jnp.where(picked[:, :, None], pairs[None], 0.0), axis=1)

    def reduce(best):
        parts = best.astype(wire)
        mine = parts[0]
        for step in range(chips - 1, 0, -1):
            pairs = [(2 * z + c, 2 * mate(z, step, chips) + c) for z in range(chips) for c in range(2)]
            mine = jnp.maximum(mine, lax.ppermute(parts[step], "ctrl", pairs))
        return mine

    def gather(mine):
        pieces = []
        for step in range(chips - 1, 0, -1):
            pairs = [(2 * mate(z, step, chips) + c, 2 * z + c) for z in range(chips) for c in range(2)]
            pieces.append(lax.ppermute(mine, "ctrl", pairs))
        return jnp.stack([mine, *pieces[::-1]])

    steps = sum(half + SUBSTEPS - 2 - 2 * k for k in range(SUBSTEPS))
    early_out = [shape(chips, half - SUBSTEPS, width, nz)] + keeps
    rest_out = shape(chips, SUBSTEPS, width, nz)
    rest_rows, rest_steps = 2 * SUBSTEPS + 2, SUBSTEPS * SUBSTEPS

    best, keep_a, keep_b, speed_rows, reward_rows = call(
        early_first,
        rows,
        steps,
        (block, speed, reward, other),
        early_out + [shape(given, ny, nz), shape(count, given, ny, nz)],
    )
    laid, edges = (speed_rows, reward_rows), (edge, edge_other)
    best_rest = call(rest_first, rest_rows, rest_steps, (block, *laid, *edges, keep_a, keep_b), rest_out)
    pieces = gather(reduce(jnp.concatenate([best_rest, best], axis=1)))

    across = lax.ppermute(pieces[:, -SUBSTEPS:], "ctrl", partners)
    beyond = lax.ppermute(pieces[:, :SUBSTEPS].astype(narrow), both, facing)
    current = pieces.astype(jnp.float32)
    best, *kept = call(early_later, rows, steps, (current, across.astype(jnp.float32), *laid), early_out)
    best_rest = call(
        rest_later, rest_rows, rest_steps, (current, beyond, *laid, *edges, *kept), rest_out
    )
    pieces = gather(reduce(jnp.concatenate([best_rest, best], axis=1)))

    from_partner = lax.ppermute(pieces, "ctrl", partners)

    def in_order(parts, flipped):
        ordered = [
            lax.dynamic_index_in_dim(parts, mate_step(chip, shard, chips), 0, keepdims=False) for shard in range(chips)
        ]
        block_rows = jnp.concatenate(ordered, axis=1)
        return jnp.where(flipped, block_rows[::-1], block_rows).astype(jnp.float32)

    result = jnp.zeros((cells, ny, nz), jnp.float32)
    result = lax.dynamic_update_slice_in_dim(result, in_order(pieces, upper == 1), upper * half, axis=0)
    return lax.dynamic_update_slice_in_dim(result, in_order(from_partner, upper == 0), (1 - upper) * half, axis=0)


def solution(mesh):
    in_specs = (
        P("slab", None, None),
        P("slab", None, None),
        P("ctrl", "slab", None, None),
        P("ctrl"),
        P(),
        P(),
    )
    out_specs = P("slab", None, None)
    return jax.shard_map(body, mesh=mesh, in_specs=in_specs, out_specs=out_specs, check_vma=False)
```

```python
import functools

import jax
import jax.numpy as jnp
from jax import lax
from jax.experimental import pallas as pl
from jax.experimental.pallas import tpu as pltpu
from jax.sharding import PartitionSpec as P

SUBSTEPS = 3
PAD = 8
CHUNK = 32
LOWEST = -3.0e38
WIRE_SCALE = 4096.0


def mate(chip, step, chips):
    if chips & (chips - 1) == 0:
        return chip ^ step
    return (chip + step) % chips


def mate_step(chip, other, chips):
    if chips & (chips - 1) == 0:
        return chip ^ other
    return (other - chip) % chips


def where_am_i():
    slab, member = lax.axis_index("slab"), lax.axis_index("ctrl")
    upper = (member + slab) % 2
    end = jnp.where(upper == 0, 0, lax.axis_size("slab") - 1)
    return member // 2, upper, jnp.where(slab == end, 0, 1)


def coefficients(coef, ctrl):
    rates = [coef[ctrl, dim] for dim in range(3)]
    drifts = [coef[ctrl, 3 + dim] for dim in range(3)]
    sizes = [jnp.maximum(drift, -drift) for drift in drifts]
    return rates, sizes, 1.0 - 2.0 * (rates[0] + rates[1] + rates[2]), sizes[0] + sizes[1] + sizes[2], drifts


def taps(src, rows, first, size):
    lines = pl.ds(PAD + first, size)
    behind, center = src[rows[0] - 1, lines, :], src[rows[0], lines, :]
    nz = center.shape[1]
    lane = lax.broadcasted_iota(jnp.int32, center.shape, 1)
    for row in rows:
        ahead = src[row + 1, lines, :]
        y_ahead = src[row, pl.ds(PAD + first + 1, size), :]
        y_behind = src[row, pl.ds(PAD + first - 1, size), :]
        z_ahead = jnp.where(lane == nz - 1, 0.0, pltpu.roll(center, nz - 1, 1))
        z_behind = jnp.where(lane == 0, 0.0, pltpu.roll(center, 1, 1))
        yield row, center, ((ahead, behind), (y_ahead, y_behind), (z_ahead, z_behind))
        behind, center = center, ahead


def blend(coef, ups, center, sides, sums, speed, reward):
    rates, sizes, weight, size, _ = coef
    winds = [jnp.where(up, *side) for up, side in zip(ups, sides)]
    still = reward + weight * center + rates[0] * sums[0]
    still = still + rates[1] * sums[1] + rates[2] * sums[2]
    wind = sizes[0] * winds[0] + sizes[1] * winds[1] + sizes[2] * winds[2]
    return still + speed * (wind - size * center)


def sweep(place, coef, ctrls, src, rows, speed, reward, store):
    ny = src.shape[1] - 2 * PAD
    coefs = [coefficients(coef, ctrl) for ctrl in ctrls]
    ups = [winds_of(place, own_coef[4]) for own_coef in coefs]
    size = min(ny, CHUNK)
    for first in range(0, ny, size):
        spot = pl.ds(first, size)
        for row, center, sides in taps(src, rows, first, size):
            sums = [ahead + behind for ahead, behind in sides]
            pace = speed(row, spot)
            for ctrl, own_coef, up in zip(ctrls, coefs, ups):
                store(ctrl, row, first, size, blend(own_coef, up, center, sides, sums, pace, reward(ctrl, row, spot)))


def winds_of(place, drifts):
    x_up = jnp.where(place[1] == 0, drifts[0], -drifts[0]) > 0.0
    return x_up, drifts[1] > 0.0, drifts[2] > 0.0


def put_max(place, out, index, first, new):
    chips, width = out.shape[0], out.shape[2]
    size = min(width, new.shape[0])
    for part in range(0, new.shape[0], size):
        spot = mate_step(place[0], (first + part) // width, chips)
        lines = pl.ds((first + part) % width, size)
        out[spot, index, lines, :] = jnp.maximum(out[spot, index, lines, :], new[part : part + size])


def start_max(out):
    for shard in range(out.shape[0]):
        for row in range(out.shape[1]):
            out[shard, row] = jnp.full(out.shape[2:], LOWEST, out.dtype)


def clear_pads(field, ny):
    if len(field.shape) > 3:
        for part in range(field.shape[0]):
            clear_pads(field.at[part], ny)
        return
    zero = jnp.zeros((PAD, field.shape[2]), field.dtype)
    for row in range(field.shape[0]):
        field[row, 0:PAD, :] = zero
        field[row, PAD + ny : 2 * PAD + ny, :] = zero


def lay_rows(place, speed, reward, other, speed_rows, reward_rows):
    own, cells = reward.shape[:2]
    for q in range(speed_rows.shape[0]):
        real = jnp.where(place[1] == 0, q, cells - 1 - q)
        speed_rows[q] = speed[real]
        for ctrl in range(own):
            reward_rows[ctrl, q] = reward[ctrl, real].astype(jnp.float32)
            reward_rows[own + ctrl, q] = other[ctrl, real].astype(jnp.float32)


def lay_lower(edge, edge_other, lower_rows):
    mine = edge_other.shape[0]
    for row in range(mine):
        lower_rows[row] = edge[edge.shape[0] - mine + row]
        lower_rows[mine + row] = edge_other[row]


def spread(place, pieces, index, field, row):
    chips, width = pieces.shape[0], pieces.shape[2]
    for shard in range(chips):
        piece = pieces[mate_step(place[0], shard, chips), index]
        field[row, pl.ds(PAD + shard * width, width), :] = piece.astype(field.dtype)


def early_march(place, coef, half, block, speed_rows, reward_rows, out, keeps, fields):
    count = reward_rows.shape[0]
    start_max(out)

    def speed(q, spot):
        return speed_rows[q, spot, :]

    def reward(ctrl, q, spot):
        return reward_rows[ctrl, q, spot, :]

    def keep(substep, ctrl, q, first, size, new):
        if q < substep + 3:
            keeps[substep][ctrl, q - substep - 1, pl.ds(first, size), :] = new

    def store(ctrl, q, first, size, new):
        fields[0][ctrl, q, pl.ds(PAD + first, size), :] = new
        keep(0, ctrl, q, first, size, new)

    sweep(place, coef, range(count), block, range(1, half + SUBSTEPS - 1), speed, reward, store)

    def one(ctrl, carry):
        source = fields[0].at[ctrl]
        for substep in range(1, SUBSTEPS):
            last = substep == SUBSTEPS - 1

            def store(ctrl, q, first, size, new, substep=substep, last=last):
                if last:
                    put_max(place, out, q - SUBSTEPS, first, new)
                    return
                fields[substep][q, pl.ds(PAD + first, size), :] = new
                keep(substep, ctrl, q, first, size, new)

            rows = range(1 + substep, half + SUBSTEPS - 1 - substep)
            sweep(place, coef, [ctrl], source, rows, speed, reward, store)
            source = None if last else fields[substep]
        return carry

    lax.fori_loop(0, count, one, 0)


def rest_march(place, coef, edge, lower_rows, block, speed_rows, reward_rows, out, keeps, fields):
    ny = block.shape[1] - 2 * PAD
    count = reward_rows.shape[0]
    margin = SUBSTEPS - 1
    inside = place[2].astype(jnp.float32)
    start_max(out)

    def speed(row, spot):
        q = row - SUBSTEPS
        if q < 0:
            return edge[SUBSTEPS - 1 - q, spot, :].astype(jnp.float32)
        return speed_rows[q, spot, :]

    def reward(ctrl, row, spot):
        q = row - SUBSTEPS
        if q < 0:
            return lower_rows[ctrl * margin - 1 - q, spot, :].astype(jnp.float32)
        return reward_rows[ctrl, q, spot, :]

    def store(ctrl, row, first, size, new):
        fields[0][ctrl, row, pl.ds(PAD + first, size), :] = new * inside if row < SUBSTEPS else new

    sweep(place, coef, range(count), block, range(1, SUBSTEPS + 1), speed, reward, store)

    def one(ctrl, carry):
        source = fields[0].at[ctrl]
        for substep in range(1, SUBSTEPS):
            last = substep == SUBSTEPS - 1
            for kept in range(2):
                source[substep + kept + SUBSTEPS, pl.ds(PAD, ny), :] = keeps[substep - 1][ctrl, kept]

            def store(ctrl, row, first, size, new, substep=substep, last=last):
                if last:
                    put_max(place, out, row - SUBSTEPS, first, new)
                    return
                new = new * inside if row < SUBSTEPS else new
                fields[substep][row, pl.ds(PAD + first, size), :] = new

            rows = range(1 + substep, SUBSTEPS + 1 + substep)
            sweep(place, coef, [ctrl], source, rows, speed, reward, store)
            source = None if last else fields[substep]
        return carry

    lax.fori_loop(0, count, one, 0)


def pack_kernel(value, speed, reward, edge, far, block, speed_rows, value_sem, speed_sem, near_sem, far_sem):
    place = where_am_i()
    cells, ny = value.shape[:2]
    own = reward.shape[0]
    margin = SUBSTEPS - 1
    copies, later = [], []
    for row in range(SUBSTEPS):
        near = jnp.where(place[1] == 0, row, cells - 1 - row)
        away = jnp.where(place[1] == 0, cells - 1 - row, row)
        copies.append(pltpu.make_async_copy(value.at[near], block.at[row, pl.ds(PAD, ny)], value_sem.at[row]))
        if row < margin:
            copies.append(pltpu.make_async_copy(speed.at[near], speed_rows.at[row], speed_sem.at[row]))
            for ctrl in range(own):
                spot = ctrl * margin + row
                place_near = edge.at[SUBSTEPS + margin + spot]
                later.append(pltpu.make_async_copy(reward.at[ctrl, near], place_near, near_sem.at[spot]))
                later.append(pltpu.make_async_copy(reward.at[ctrl, away], far.at[spot], far_sem.at[spot]))
    for row in range(SUBSTEPS, block.shape[0]):
        real = jnp.where(place[1] == 0, row, cells - 1 - row)
        later.append(pltpu.make_async_copy(value.at[real], block.at[row, pl.ds(PAD, ny)], value_sem.at[row]))
    for copy in copies + later:
        copy.start()
    clear_pads(block, ny)
    for copy in copies:
        copy.wait()
    for row in range(SUBSTEPS):
        edge[row] = block[row, pl.ds(PAD, ny), :].astype(edge.dtype)
    for row in range(margin):
        edge[SUBSTEPS + row] = speed_rows[row].astype(edge.dtype)
    for copy in later:
        copy.wait()


def early_first(coef, block, speed, reward, other, out, *refs, half):
    keeps, (speed_rows, reward_rows), fields = refs[:2], refs[2:4], refs[4:]
    place = where_am_i()
    for field in fields:
        clear_pads(field, speed.shape[1])
    lay_rows(place, speed, reward, other, speed_rows, reward_rows)
    early_march(place, coef, half, block, speed_rows, reward_rows, out, keeps, fields)


def rest_first(coef, first, speed_rows, reward_rows, edge, *refs, half):
    edge_other, keeps, out, fields, block, lower_rows = refs[0], refs[1:3], refs[3], refs[4:6], refs[6], refs[7]
    place = where_am_i()
    ny = speed_rows.shape[1]
    for field in (block, *fields):
        clear_pads(field, ny)
    for row in range(SUBSTEPS):
        block[SUBSTEPS - 1 - row, pl.ds(PAD, ny), :] = edge[row].astype(jnp.float32)
    for row in range(2):
        block[SUBSTEPS + row] = first[row]
    lay_lower(edge, edge_other, lower_rows)
    rest_march(place, coef, edge, lower_rows, block, speed_rows, reward_rows, out, keeps, fields)


def early_later(coef, current, across, speed_rows, reward_rows, out, *refs, half):
    keeps, fields, block = refs[:2], refs[2:4], refs[4]
    place = where_am_i()
    for field in (block, *fields):
        clear_pads(field, speed_rows.shape[1])
    for q in range(half):
        spread(place, current, q, block, q)
    for row in range(SUBSTEPS):
        spread(place, across, SUBSTEPS - 1 - row, block, half + row)
    early_march(place, coef, half, block, speed_rows, reward_rows, out, keeps, fields)


def rest_later(coef, current, beyond, speed_rows, reward_rows, edge, *refs, half):
    edge_other, keeps, out, fields, block, lower_rows = refs[0], refs[1:3], refs[3], refs[4:6], refs[6], refs[7]
    place = where_am_i()
    for field in (block, *fields):
        clear_pads(field, speed_rows.shape[1])
    for row in range(SUBSTEPS):
        spread(place, beyond, row, block, SUBSTEPS - 1 - row)
    for row in range(2):
        spread(place, current, row, block, SUBSTEPS + row)
    lay_lower(edge, edge_other, lower_rows)
    rest_march(place, coef, edge, lower_rows, block, speed_rows, reward_rows, out, keeps, fields)


def body(value, speed, reward, ctrl_set, drift_sets, diffusion_sets):
    own, cells, ny, nz = reward.shape
    count = 2 * own
    slabs, members = lax.axis_size("slab"), lax.axis_size("ctrl")
    chips, half = members // 2, cells // 2
    width = ny // chips
    chip, upper, _ = where_am_i()
    margin = SUBSTEPS - 1
    narrow, wire = jnp.bfloat16, jnp.float16
    both = ("slab", "ctrl")

    def device(s, z, c):
        return s * members + 2 * z + c

    partners = [(i, i ^ 1) for i in range(members)]

    facing, beside = [], []
    for s in range(slabs - 1):
        for z in range(chips):
            c = (s + 1) % 2
            facing += [(device(s, z, c), device(s + 1, z, c)), (device(s + 1, z, c), device(s, z, c))]
            beside += [(device(s, z, 1 - c), device(s + 1, z, c)), (device(s + 1, z, 1 - c), device(s, z, c))]

    whole = pl.BlockSpec(memory_space=pltpu.VMEM)
    scalars = pl.BlockSpec(memory_space=pltpu.SMEM)

    def shape(*dims):
        return jax.ShapeDtypeStruct(dims, jnp.float32)

    def call(kernel, rows, marched, arrays, outs):
        field = pltpu.VMEM((rows, ny + 2 * PAD, nz), jnp.float32)
        scratch = [pltpu.VMEM((count, rows, ny + 2 * PAD, nz), jnp.float32)] + [field] * (SUBSTEPS - 2)
        if kernel is not early_first:
            scratch.append(field)
        if kernel in (rest_first, rest_later):
            scratch.append(pltpu.VMEM((count * margin, ny, nz), narrow))
        return pl.pallas_call(
            functools.partial(kernel, half=half),
            out_shape=outs,
            in_specs=[scalars] + [whole] * len(arrays),
            out_specs=jax.tree.map(lambda _: whole, outs),
            scratch_shapes=scratch,
            compiler_params=pltpu.CompilerParams(vmem_limit_bytes=16 * 2**20),
            cost_estimate=pl.CostEstimate(
                flops=25 * count * marched * ny * nz, bytes_accessed=12 * count * marched * ny * nz, transcendentals=0
            ),
        )(coef, *arrays)

    keeps = [shape(count, 2, ny, nz)] * (SUBSTEPS - 1)

    rows, given = half + SUBSTEPS, half + margin
    other_set = lax.ppermute(ctrl_set, "ctrl", partners)
    other = lax.ppermute(reward, "ctrl", partners)
    anywhere = pl.BlockSpec(memory_space=pl.ANY)
    dma = pltpu.SemaphoreType.DMA
    packed, far, block = pl.pallas_call(
        pack_kernel,
        out_shape=[
            pltpu.VMEM((SUBSTEPS + margin + own * margin, ny, nz), narrow),
            pltpu.VMEM((own * margin, ny, nz), narrow),
            pltpu.VMEM((rows, ny + 2 * PAD, nz), jnp.float32),
        ],
        in_specs=[anywhere] * 3,
        out_specs=[whole] * 3,
        scratch_shapes=[
            pltpu.VMEM((margin, ny, nz), jnp.float32),
            dma((rows,)),
            dma((margin,)),
            dma((own * margin,)),
            dma((own * margin,)),
        ],
    )(value, speed, reward)
    packed, far, other_set = lax.optimization_barrier((packed, far, other_set))
    edge = lax.ppermute(packed, both, facing)
    edge_other = lax.ppermute(far, both, beside)

    sets = jnp.concatenate([ctrl_set, other_set])
    picked = sets[:, None] == jnp.arange(drift_sets.shape[0], dtype=jnp.int32)[None, :]
    pairs = jnp.concatenate([diffusion_sets, drift_sets], axis=1)
    coef = jnp.sum(jnp.where(picked[:, :, None], pairs[None], 0.0), axis=1)

    def from_wire(values):
        return values.astype(jnp.float32) * (1.0 / WIRE_SCALE)

    def reduce(best):
        parts = (best * WIRE_SCALE).astype(wire)
        mine = parts[0]
        for step in range(chips - 1, 0, -1):
            pairs = [(2 * z + c, 2 * mate(z, step, chips) + c) for z in range(chips) for c in range(2)]
            mine = jnp.maximum(mine, lax.ppermute(parts[step], "ctrl", pairs))
        return mine

    def gather(mine):
        pieces = []
        for step in range(chips - 1, 0, -1):
            pairs = [(2 * mate(z, step, chips) + c, 2 * z + c) for z in range(chips) for c in range(2)]
            pieces.append(lax.ppermute(mine, "ctrl", pairs))
        return jnp.stack([mine, *pieces[::-1]])

    steps = sum(half + SUBSTEPS - 2 - 2 * k for k in range(SUBSTEPS))
    early_out = [shape(chips, half - SUBSTEPS, width, nz)] + keeps
    rest_out = shape(chips, SUBSTEPS, width, nz)
    rest_rows, rest_steps = 2 * SUBSTEPS + 2, SUBSTEPS * SUBSTEPS

    best, keep_a, keep_b, speed_rows, reward_rows = call(
        early_first,
        rows,
        steps,
        (block, speed, reward, other),
        early_out + [shape(given, ny, nz), shape(count, given, ny, nz)],
    )
    laid, edges = (speed_rows, reward_rows), (edge, edge_other)
    best_rest = call(rest_first, rest_rows, rest_steps, (block, *laid, *edges, keep_a, keep_b), rest_out)
    pieces = gather(reduce(jnp.concatenate([best_rest, best], axis=1)))

    across = lax.ppermute(pieces[:, -SUBSTEPS:], "ctrl", partners)
    beyond = lax.ppermute(from_wire(pieces[:, :SUBSTEPS]).astype(narrow), both, facing)
    current = from_wire(pieces)
    best, *kept = call(early_later, rows, steps, (current, from_wire(across), *laid), early_out)
    best_rest = call(
        rest_later, rest_rows, rest_steps, (current, beyond, *laid, *edges, *kept), rest_out
    )
    pieces = gather(reduce(jnp.concatenate([best_rest, best], axis=1)))

    from_partner = lax.ppermute(pieces, "ctrl", partners)

    def in_order(parts, flipped):
        ordered = [
            lax.dynamic_index_in_dim(parts, mate_step(chip, shard, chips), 0, keepdims=False) for shard in range(chips)
        ]
        block_rows = jnp.concatenate(ordered, axis=1)
        return from_wire(jnp.where(flipped, block_rows[::-1], block_rows))

    result = jnp.zeros((cells, ny, nz), jnp.float32)
    result = lax.dynamic_update_slice_in_dim(result, in_order(pieces, upper == 1), upper * half, axis=0)
    return lax.dynamic_update_slice_in_dim(result, in_order(from_partner, upper == 0), (1 - upper) * half, axis=0)


def solution(mesh):
    in_specs = (
        P("slab", None, None),
        P("slab", None, None),
        P("ctrl", "slab", None, None),
        P("ctrl"),
        P(),
        P(),
    )
    out_specs = P("slab", None, None)
    return jax.shard_map(body, mesh=mesh, in_specs=in_specs, out_specs=out_specs, check_vma=False)
```

```python
import functools

import jax
import jax.numpy as jnp
from jax import lax
from jax.experimental import pallas as pl
from jax.experimental.pallas import tpu as pltpu
from jax.sharding import PartitionSpec as P

SUBSTEPS = 3
PAD = 8
CHUNK = 32
LOWEST = -3.0e38
WIRE_SCALE = 4096.0


def mate(chip, step, chips):
    if chips & (chips - 1) == 0:
        return chip ^ step
    return (chip + step) % chips


def mate_step(chip, other, chips):
    if chips & (chips - 1) == 0:
        return chip ^ other
    return (other - chip) % chips


def where_am_i():
    slab, member = lax.axis_index("slab"), lax.axis_index("ctrl")
    upper = (member + slab) % 2
    end = jnp.where(upper == 0, 0, lax.axis_size("slab") - 1)
    return member // 2, upper, jnp.where(slab == end, 0, 1)


def coefficients(coef, ctrl):
    rates = [coef[ctrl, dim] for dim in range(3)]
    drifts = [coef[ctrl, 3 + dim] for dim in range(3)]
    sizes = [jnp.maximum(drift, -drift) for drift in drifts]
    return rates, sizes, 1.0 - 2.0 * (rates[0] + rates[1] + rates[2]), sizes[0] + sizes[1] + sizes[2], drifts


def taps(src, rows, first, size):
    lines = pl.ds(PAD + first, size)
    behind, center = src[rows[0] - 1, lines, :], src[rows[0], lines, :]
    nz = center.shape[1]
    lane = lax.broadcasted_iota(jnp.int32, center.shape, 1)
    for row in rows:
        ahead = src[row + 1, lines, :]
        y_ahead = src[row, pl.ds(PAD + first + 1, size), :]
        y_behind = src[row, pl.ds(PAD + first - 1, size), :]
        z_ahead = jnp.where(lane == nz - 1, 0.0, pltpu.roll(center, nz - 1, 1))
        z_behind = jnp.where(lane == 0, 0.0, pltpu.roll(center, 1, 1))
        yield row, center, ((ahead, behind), (y_ahead, y_behind), (z_ahead, z_behind))
        behind, center = center, ahead


def blend(coef, ups, center, sides, sums, speed, reward):
    rates, sizes, weight, size, _ = coef
    winds = [jnp.where(up, *side) for up, side in zip(ups, sides)]
    still = reward + weight * center + rates[0] * sums[0]
    still = still + rates[1] * sums[1] + rates[2] * sums[2]
    wind = sizes[0] * winds[0] + sizes[1] * winds[1] + sizes[2] * winds[2]
    return still + speed * (wind - size * center)


def sweep(place, coef, ctrls, src, rows, speed, reward, store):
    ny = src.shape[1] - 2 * PAD
    coefs = [coefficients(coef, ctrl) for ctrl in ctrls]
    ups = [winds_of(place, own_coef[4]) for own_coef in coefs]
    size = min(ny, CHUNK)
    for first in range(0, ny, size):
        spot = pl.ds(first, size)
        for row, center, sides in taps(src, rows, first, size):
            sums = [ahead + behind for ahead, behind in sides]
            pace = speed(row, spot)
            for ctrl, own_coef, up in zip(ctrls, coefs, ups):
                store(ctrl, row, first, size, blend(own_coef, up, center, sides, sums, pace, reward(ctrl, row, spot)))


def winds_of(place, drifts):
    x_up = jnp.where(place[1] == 0, drifts[0], -drifts[0]) > 0.0
    return x_up, drifts[1] > 0.0, drifts[2] > 0.0


def put_max(place, out, index, first, new):
    chips, width = out.shape[0], out.shape[2]
    size = min(width, new.shape[0])
    for part in range(0, new.shape[0], size):
        spot = mate_step(place[0], (first + part) // width, chips)
        lines = pl.ds((first + part) % width, size)
        out[spot, index, lines, :] = jnp.maximum(out[spot, index, lines, :], new[part : part + size])


def start_max(out):
    for shard in range(out.shape[0]):
        for row in range(out.shape[1]):
            out[shard, row] = jnp.full(out.shape[2:], LOWEST, out.dtype)


def clear_pads(field, ny):
    if len(field.shape) > 3:
        for part in range(field.shape[0]):
            clear_pads(field.at[part], ny)
        return
    zero = jnp.zeros((PAD, field.shape[2]), field.dtype)
    for row in range(field.shape[0]):
        field[row, 0:PAD, :] = zero
        field[row, PAD + ny : 2 * PAD + ny, :] = zero


def lay_rows(place, speed, reward, other, speed_rows, reward_rows):
    own, cells = reward.shape[:2]
    for q in range(speed_rows.shape[0]):
        real = jnp.where(place[1] == 0, q, cells - 1 - q)
        speed_rows[q] = speed[real]
        for ctrl in range(own):
            reward_rows[ctrl, q] = reward[ctrl, real].astype(jnp.float32)
            reward_rows[own + ctrl, q] = other[ctrl, real].astype(jnp.float32)


def lay_lower(edge, edge_other, lower_rows):
    mine = edge_other.shape[0]
    for row in range(mine):
        lower_rows[row] = edge[edge.shape[0] - mine + row]
        lower_rows[mine + row] = edge_other[row]


def spread(place, pieces, index, field, row):
    chips, width = pieces.shape[0], pieces.shape[2]
    for shard in range(chips):
        piece = pieces[mate_step(place[0], shard, chips), index]
        field[row, pl.ds(PAD + shard * width, width), :] = piece.astype(field.dtype)


def early_march(place, coef, half, block, speed_rows, reward_rows, out, keeps, fields):
    count = reward_rows.shape[0]
    start_max(out)

    def speed(q, spot):
        return speed_rows[q, spot, :]

    def reward(ctrl, q, spot):
        return reward_rows[ctrl, q, spot, :]

    def keep(substep, ctrl, q, first, size, new):
        if q < substep + 3:
            keeps[substep][ctrl, q - substep - 1, pl.ds(first, size), :] = new

    def store(ctrl, q, first, size, new):
        fields[0][ctrl, q, pl.ds(PAD + first, size), :] = new
        keep(0, ctrl, q, first, size, new)

    sweep(place, coef, range(count), block, range(1, half + SUBSTEPS - 1), speed, reward, store)

    def one(ctrl, carry):
        source = fields[0].at[ctrl]
        for substep in range(1, SUBSTEPS):
            last = substep == SUBSTEPS - 1

            def store(ctrl, q, first, size, new, substep=substep, last=last):
                if last:
                    put_max(place, out, q - SUBSTEPS, first, new)
                    return
                fields[substep][q, pl.ds(PAD + first, size), :] = new
                keep(substep, ctrl, q, first, size, new)

            rows = range(1 + substep, half + SUBSTEPS - 1 - substep)
            sweep(place, coef, [ctrl], source, rows, speed, reward, store)
            source = None if last else fields[substep]
        return carry

    lax.fori_loop(0, count, one, 0)


def rest_march(place, coef, ctrls, edge, lower_rows, block, speed_rows, reward_rows, out, keeps, fields):
    ny = block.shape[1] - 2 * PAD
    margin = SUBSTEPS - 1
    inside = place[2].astype(jnp.float32)

    def speed(row, spot):
        q = row - SUBSTEPS
        if q < 0:
            return edge[SUBSTEPS - 1 - q, spot, :].astype(jnp.float32)
        return speed_rows[q, spot, :]

    def reward(ctrl, row, spot):
        q = row - SUBSTEPS
        if q < 0:
            return lower_rows[(ctrl - ctrls[0]) * margin - 1 - q, spot, :].astype(jnp.float32)
        return reward_rows[ctrl, q, spot, :]

    def store(ctrl, row, first, size, new):
        fields[0][ctrl, row, pl.ds(PAD + first, size), :] = new * inside if row < SUBSTEPS else new

    sweep(place, coef, ctrls, block, range(1, SUBSTEPS + 1), speed, reward, store)

    def one(ctrl, carry):
        source = fields[0].at[ctrl]
        for substep in range(1, SUBSTEPS):
            last = substep == SUBSTEPS - 1
            for kept in range(2):
                source[substep + kept + SUBSTEPS, pl.ds(PAD, ny), :] = keeps[substep - 1][ctrl, kept]

            def store(ctrl, row, first, size, new, substep=substep, last=last):
                if last:
                    put_max(place, out, row - SUBSTEPS, first, new)
                    return
                new = new * inside if row < SUBSTEPS else new
                fields[substep][row, pl.ds(PAD + first, size), :] = new

            rows = range(1 + substep, SUBSTEPS + 1 + substep)
            sweep(place, coef, [ctrl], source, rows, speed, reward, store)
            source = None if last else fields[substep]
        return carry

    lax.fori_loop(ctrls[0], ctrls[-1] + 1, one, 0)


def pack_kernel(value, speed, reward, edge, far, block, speed_rows, value_sem, speed_sem, near_sem, far_sem):
    place = where_am_i()
    cells, ny = value.shape[:2]
    own = reward.shape[0]
    margin = SUBSTEPS - 1
    copies, later = [], []
    for row in range(SUBSTEPS):
        near = jnp.where(place[1] == 0, row, cells - 1 - row)
        away = jnp.where(place[1] == 0, cells - 1 - row, row)
        copies.append(pltpu.make_async_copy(value.at[near], block.at[row, pl.ds(PAD, ny)], value_sem.at[row]))
        if row < margin:
            copies.append(pltpu.make_async_copy(speed.at[near], speed_rows.at[row], speed_sem.at[row]))
            for ctrl in range(own):
                spot = ctrl * margin + row
                place_near = edge.at[SUBSTEPS + margin + spot]
                later.append(pltpu.make_async_copy(reward.at[ctrl, near], place_near, near_sem.at[spot]))
                later.append(pltpu.make_async_copy(reward.at[ctrl, away], far.at[spot], far_sem.at[spot]))
    for row in range(SUBSTEPS, block.shape[0]):
        real = jnp.where(place[1] == 0, row, cells - 1 - row)
        later.append(pltpu.make_async_copy(value.at[real], block.at[row, pl.ds(PAD, ny)], value_sem.at[row]))
    for copy in copies + later:
        copy.start()
    clear_pads(block, ny)
    for copy in copies:
        copy.wait()
    for row in range(SUBSTEPS):
        edge[row] = block[row, pl.ds(PAD, ny), :].astype(edge.dtype)
    for row in range(margin):
        edge[SUBSTEPS + row] = speed_rows[row].astype(edge.dtype)
    for copy in later:
        copy.wait()


def early_first(coef, block, speed, reward, other, out, *refs, half):
    keeps, (speed_rows, reward_rows), fields = refs[:2], refs[2:4], refs[4:]
    place = where_am_i()
    for field in fields:
        clear_pads(field, speed.shape[1])
    lay_rows(place, speed, reward, other, speed_rows, reward_rows)
    early_march(place, coef, half, block, speed_rows, reward_rows, out, keeps, fields)


def rest_first(coef, first, speed_rows, reward_rows, edge, *refs, half):
    *others, keep_a, keep_b, out, field_a, field_b, block = refs
    place = where_am_i()
    ny = speed_rows.shape[1]
    own = reward_rows.shape[0] // 2
    for field in (field_a.at[pl.ds(own if others else 0, own)], field_b, block):
        clear_pads(field, ny)
    for row in range(SUBSTEPS):
        block[SUBSTEPS - 1 - row, pl.ds(PAD, ny), :] = edge[row].astype(jnp.float32)
    for row in range(2):
        block[SUBSTEPS + row] = first[row]
    if others:
        lower_rows, best = others
        ctrls = range(own, 2 * own)
        for shard in range(out.shape[0]):
            out[shard] = best[shard]
    else:
        lower_rows, ctrls = edge.at[pl.ds(2 * SUBSTEPS - 1, own * (SUBSTEPS - 1))], range(own)
        start_max(out)
    keeps, fields = (keep_a, keep_b), (field_a, field_b)
    rest_march(place, coef, ctrls, edge, lower_rows, block, speed_rows, reward_rows, out, keeps, fields)


def early_later(coef, current, across, speed_rows, reward_rows, out, *refs, half):
    keeps, fields, block = refs[:2], refs[2:4], refs[4]
    place = where_am_i()
    for field in (block, *fields):
        clear_pads(field, speed_rows.shape[1])
    for q in range(half):
        spread(place, current, q, block, q)
    for row in range(SUBSTEPS):
        spread(place, across, SUBSTEPS - 1 - row, block, half + row)
    early_march(place, coef, half, block, speed_rows, reward_rows, out, keeps, fields)


def rest_later(coef, current, beyond, speed_rows, reward_rows, edge, *refs, half):
    edge_other, keeps, out, fields, block, lower_rows = refs[0], refs[1:3], refs[3], refs[4:6], refs[6], refs[7]
    place = where_am_i()
    for field in (block, *fields):
        clear_pads(field, speed_rows.shape[1])
    for row in range(SUBSTEPS):
        spread(place, beyond, row, block, SUBSTEPS - 1 - row)
    for row in range(2):
        spread(place, current, row, block, SUBSTEPS + row)
    lay_lower(edge, edge_other, lower_rows)
    start_max(out)
    ctrls = range(reward_rows.shape[0])
    rest_march(place, coef, ctrls, edge, lower_rows, block, speed_rows, reward_rows, out, keeps, fields)


def body(value, speed, reward, ctrl_set, drift_sets, diffusion_sets):
    own, cells, ny, nz = reward.shape
    count = 2 * own
    slabs, members = lax.axis_size("slab"), lax.axis_size("ctrl")
    chips, half = members // 2, cells // 2
    width = ny // chips
    chip, upper, _ = where_am_i()
    margin = SUBSTEPS - 1
    narrow, wire = jnp.bfloat16, jnp.float16
    both = ("slab", "ctrl")

    def device(s, z, c):
        return s * members + 2 * z + c

    partners = [(i, i ^ 1) for i in range(members)]

    facing, beside = [], []
    for s in range(slabs - 1):
        for z in range(chips):
            c = (s + 1) % 2
            facing += [(device(s, z, c), device(s + 1, z, c)), (device(s + 1, z, c), device(s, z, c))]
            beside += [(device(s, z, 1 - c), device(s + 1, z, c)), (device(s + 1, z, 1 - c), device(s, z, c))]

    whole = pl.BlockSpec(memory_space=pltpu.VMEM)
    scalars = pl.BlockSpec(memory_space=pltpu.SMEM)

    def shape(*dims):
        return jax.ShapeDtypeStruct(dims, jnp.float32)

    def call(kernel, rows, marched, arrays, outs):
        field = pltpu.VMEM((rows, ny + 2 * PAD, nz), jnp.float32)
        scratch = [pltpu.VMEM((count, rows, ny + 2 * PAD, nz), jnp.float32)] + [field] * (SUBSTEPS - 2)
        if kernel is not early_first:
            scratch.append(field)
        if kernel is rest_later:
            scratch.append(pltpu.VMEM((count * margin, ny, nz), narrow))
        return pl.pallas_call(
            functools.partial(kernel, half=half),
            out_shape=outs,
            in_specs=[scalars] + [whole] * len(arrays),
            out_specs=jax.tree.map(lambda _: whole, outs),
            scratch_shapes=scratch,
            compiler_params=pltpu.CompilerParams(vmem_limit_bytes=16 * 2**20),
            cost_estimate=pl.CostEstimate(
                flops=25 * count * marched * ny * nz, bytes_accessed=12 * count * marched * ny * nz, transcendentals=0
            ),
        )(coef, *arrays)

    keeps = [shape(count, 2, ny, nz)] * (SUBSTEPS - 1)

    rows, given = half + SUBSTEPS, half + margin
    other_set = lax.ppermute(ctrl_set, "ctrl", partners)
    other = lax.ppermute(reward, "ctrl", partners)
    anywhere = pl.BlockSpec(memory_space=pl.ANY)
    dma = pltpu.SemaphoreType.DMA
    packed, far, block = pl.pallas_call(
        pack_kernel,
        out_shape=[
            pltpu.VMEM((SUBSTEPS + margin + own * margin, ny, nz), narrow),
            pltpu.VMEM((own * margin, ny, nz), narrow),
            pltpu.VMEM((rows, ny + 2 * PAD, nz), jnp.float32),
        ],
        in_specs=[anywhere] * 3,
        out_specs=[whole] * 3,
        scratch_shapes=[
            pltpu.VMEM((margin, ny, nz), jnp.float32),
            dma((rows,)),
            dma((margin,)),
            dma((own * margin,)),
            dma((own * margin,)),
        ],
    )(value, speed, reward)
    packed, far, other_set = lax.optimization_barrier((packed, far, other_set))
    edge = lax.ppermute(packed, both, facing)
    edge_other = lax.ppermute(far, both, beside)

    sets = jnp.concatenate([ctrl_set, other_set])
    picked = sets[:, None] == jnp.arange(drift_sets.shape[0], dtype=jnp.int32)[None, :]
    pairs = jnp.concatenate([diffusion_sets, drift_sets], axis=1)
    coef = jnp.sum(jnp.where(picked[:, :, None], pairs[None], 0.0), axis=1)

    def from_wire(values):
        return values.astype(jnp.float32) * (1.0 / WIRE_SCALE)

    falling = list(range(chips - 1, 0, -1))
    turned = falling[1:-1] + falling[:1] + falling[-1:]
    odd_core = lax.axis_index("ctrl") % 2

    def reduce(best, orders):
        parts = (best * WIRE_SCALE).astype(wire)
        mine = parts[0]
        for steps_of in zip(*orders):
            pairs = [(2 * z + c, 2 * mate(z, steps_of[c], chips) + c) for z in range(chips) for c in range(2)]
            same = steps_of[0] == steps_of[1]
            part = parts[steps_of[0]] if same else jnp.where(odd_core == 0, parts[steps_of[0]], parts[steps_of[1]])
            mine = jnp.maximum(mine, lax.ppermute(part, "ctrl", pairs))
        return mine

    def gather(mine, orders):
        got = []
        for steps_of in zip(*orders):
            pairs = [(2 * mate(z, steps_of[c], chips) + c, 2 * z + c) for z in range(chips) for c in range(2)]
            got.append(lax.ppermute(mine, "ctrl", pairs))
        pieces = [mine]
        for step in range(1, chips):
            even, odd = got[orders[0].index(step)], got[orders[1].index(step)]
            pieces.append(even if even is odd else jnp.where(odd_core == 0, even, odd))
        return jnp.stack(pieces)

    steps = sum(half + SUBSTEPS - 2 - 2 * k for k in range(SUBSTEPS))
    early_out = [shape(chips, half - SUBSTEPS, width, nz)] + keeps
    rest_out = shape(chips, SUBSTEPS, width, nz)
    rest_rows, rest_steps = 2 * SUBSTEPS + 2, SUBSTEPS * SUBSTEPS

    best, keep_a, keep_b, speed_rows, reward_rows = call(
        early_first,
        rows,
        steps,
        (block, speed, reward, other),
        early_out + [shape(given, ny, nz), shape(count, given, ny, nz)],
    )
    laid, edges = (speed_rows, reward_rows), (edge, edge_other)
    best_rest = call(rest_first, rest_rows, rest_steps // 2, (block, *laid, edge, keep_a, keep_b), rest_out)
    more = (block, *laid, *edges, best_rest, keep_a, keep_b)
    best_rest = call(rest_first, rest_rows, rest_steps // 2, more, rest_out)
    pieces = gather(reduce(jnp.concatenate([best_rest, best], axis=1), (falling, turned)), (falling, turned))

    across = lax.ppermute(pieces[:, -SUBSTEPS:], "ctrl", partners)
    beyond = lax.ppermute(from_wire(pieces[:, :SUBSTEPS]).astype(narrow), both, facing)
    current = from_wire(pieces)
    best, *kept = call(early_later, rows, steps, (current, from_wire(across), *laid), early_out)
    best_rest = call(
        rest_later, rest_rows, rest_steps, (current, beyond, *laid, *edges, *kept), rest_out
    )
    pieces = gather(reduce(jnp.concatenate([best_rest, best], axis=1), (falling, turned)), (falling, turned))

    from_partner = lax.ppermute(pieces, "ctrl", partners)

    def in_order(parts, flipped):
        ordered = [
            lax.dynamic_index_in_dim(parts, mate_step(chip, shard, chips), 0, keepdims=False) for shard in range(chips)
        ]
        block_rows = jnp.concatenate(ordered, axis=1)
        return from_wire(jnp.where(flipped, block_rows[::-1], block_rows))

    result = jnp.zeros((cells, ny, nz), jnp.float32)
    result = lax.dynamic_update_slice_in_dim(result, in_order(pieces, upper == 1), upper * half, axis=0)
    return lax.dynamic_update_slice_in_dim(result, in_order(from_partner, upper == 0), (1 - upper) * half, axis=0)


def solution(mesh):
    in_specs = (
        P("slab", None, None),
        P("slab", None, None),
        P("ctrl", "slab", None, None),
        P("ctrl"),
        P(),
        P(),
    )
    out_specs = P("slab", None, None)
    return jax.shard_map(body, mesh=mesh, in_specs=in_specs, out_specs=out_specs, check_vma=False)
```

```python
import functools

import jax
import jax.numpy as jnp
from jax import lax
from jax.experimental import pallas as pl
from jax.experimental.pallas import tpu as pltpu
from jax.sharding import PartitionSpec as P

SUBSTEPS = 3
PAD = 8
CHUNK = 16
LOWEST = -3.0e38
WIRE_SCALE = 4096.0


def mate(chip, step, chips):
    if chips & (chips - 1) == 0:
        return chip ^ step
    return (chip + step) % chips


def mate_step(chip, other, chips):
    if chips & (chips - 1) == 0:
        return chip ^ other
    return (other - chip) % chips


def where_am_i():
    slab, member = lax.axis_index("slab"), lax.axis_index("ctrl")
    upper = (member + slab) % 2
    end = jnp.where(upper == 0, 0, lax.axis_size("slab") - 1)
    return member // 2, upper, jnp.where(slab == end, 0, 1)


def coefficients(coef, ctrl):
    rates = [coef[ctrl, dim] for dim in range(3)]
    drifts = [coef[ctrl, 3 + dim] for dim in range(3)]
    sizes = [jnp.maximum(drift, -drift) for drift in drifts]
    return rates, sizes, 1.0 - 2.0 * (rates[0] + rates[1] + rates[2]), sizes[0] + sizes[1] + sizes[2], drifts


def taps(src, rows, first, size):
    lines = pl.ds(PAD + first, size)
    behind, center = src[rows[0] - 1, lines, :], src[rows[0], lines, :]
    nz = center.shape[1]
    lane = lax.broadcasted_iota(jnp.int32, center.shape, 1)
    for row in rows:
        ahead = src[row + 1, lines, :]
        y_ahead = src[row, pl.ds(PAD + first + 1, size), :]
        y_behind = src[row, pl.ds(PAD + first - 1, size), :]
        z_ahead = jnp.where(lane == nz - 1, 0.0, pltpu.roll(center, nz - 1, 1))
        z_behind = jnp.where(lane == 0, 0.0, pltpu.roll(center, 1, 1))
        yield row, center, ((ahead, behind), (y_ahead, y_behind), (z_ahead, z_behind))
        behind, center = center, ahead


def blend(coef, ups, center, sides, sums, speed, reward):
    rates, sizes, weight, size, _ = coef
    winds = [jnp.where(up, *side) for up, side in zip(ups, sides)]
    still = reward + weight * center + rates[0] * sums[0]
    still = still + rates[1] * sums[1] + rates[2] * sums[2]
    wind = sizes[0] * winds[0] + sizes[1] * winds[1] + sizes[2] * winds[2]
    return still + speed * (wind - size * center)


def sweep(place, coef, ctrls, src, rows, speed, reward, store):
    ny = src.shape[1] - 2 * PAD
    coefs = [coefficients(coef, ctrl) for ctrl in ctrls]
    ups = [winds_of(place, own_coef[4]) for own_coef in coefs]
    size = min(ny, CHUNK)
    for first in range(0, ny, size):
        spot = pl.ds(first, size)
        for row, center, sides in taps(src, rows, first, size):
            sums = [ahead + behind for ahead, behind in sides]
            pace = speed(row, spot)
            for ctrl, own_coef, up in zip(ctrls, coefs, ups):
                store(ctrl, row, first, size, blend(own_coef, up, center, sides, sums, pace, reward(ctrl, row, spot)))


def winds_of(place, drifts):
    x_up = jnp.where(place[1] == 0, drifts[0], -drifts[0]) > 0.0
    return x_up, drifts[1] > 0.0, drifts[2] > 0.0


def put_max(place, out, index, first, new):
    chips, width = out.shape[0], out.shape[2]
    size = min(width, new.shape[0])
    for part in range(0, new.shape[0], size):
        spot = mate_step(place[0], (first + part) // width, chips)
        lines = pl.ds((first + part) % width, size)
        out[spot, index, lines, :] = jnp.maximum(out[spot, index, lines, :], new[part : part + size])


def start_max(out):
    for shard in range(out.shape[0]):
        for row in range(out.shape[1]):
            out[shard, row] = jnp.full(out.shape[2:], LOWEST, out.dtype)


def clear_pads(field, ny):
    if len(field.shape) > 3:
        for part in range(field.shape[0]):
            clear_pads(field.at[part], ny)
        return
    zero = jnp.zeros((PAD, field.shape[2]), field.dtype)
    for row in range(field.shape[0]):
        field[row, 0:PAD, :] = zero
        field[row, PAD + ny : 2 * PAD + ny, :] = zero


def lay_rows(place, speed, reward, other, speed_rows, reward_rows):
    own, cells = reward.shape[:2]
    for q in range(speed_rows.shape[0]):
        real = jnp.where(place[1] == 0, q, cells - 1 - q)
        speed_rows[q] = speed[real]
        for ctrl in range(own):
            reward_rows[ctrl, q] = reward[ctrl, real].astype(jnp.float32)
            reward_rows[own + ctrl, q] = other[ctrl, real].astype(jnp.float32)


def lay_lower(edge, edge_other, lower_rows):
    mine = edge_other.shape[0]
    for row in range(mine):
        lower_rows[row] = edge[edge.shape[0] - mine + row]
        lower_rows[mine + row] = edge_other[row]


def spread(place, pieces, index, field, row):
    chips, width = pieces.shape[0], pieces.shape[2]
    for shard in range(chips):
        piece = pieces[mate_step(place[0], shard, chips), index]
        field[row, pl.ds(PAD + shard * width, width), :] = piece.astype(field.dtype)


def early_march(place, coef, half, block, speed_rows, reward_rows, out, keeps, fields):
    count = reward_rows.shape[0]
    start_max(out)

    def speed(q, spot):
        return speed_rows[q, spot, :]

    def reward(ctrl, q, spot):
        return reward_rows[ctrl, q, spot, :]

    def keep(substep, ctrl, q, first, size, new):
        if q < substep + 3:
            keeps[substep][ctrl, q - substep - 1, pl.ds(first, size), :] = new

    def store(ctrl, q, first, size, new):
        fields[0][ctrl, q, pl.ds(PAD + first, size), :] = new
        keep(0, ctrl, q, first, size, new)

    sweep(place, coef, range(count), block, range(1, half + SUBSTEPS - 1), speed, reward, store)

    def one(ctrl, carry):
        source = fields[0].at[ctrl]
        for substep in range(1, SUBSTEPS):
            last = substep == SUBSTEPS - 1

            def store(ctrl, q, first, size, new, substep=substep, last=last):
                if last:
                    put_max(place, out, q - SUBSTEPS, first, new)
                    return
                fields[substep][q, pl.ds(PAD + first, size), :] = new
                keep(substep, ctrl, q, first, size, new)

            rows = range(1 + substep, half + SUBSTEPS - 1 - substep)
            sweep(place, coef, [ctrl], source, rows, speed, reward, store)
            source = None if last else fields[substep]
        return carry

    lax.fori_loop(0, count, one, 0)


def rest_march(place, coef, ctrls, edge, lower_rows, block, speed_rows, reward_rows, out, keeps, fields):
    ny = block.shape[1] - 2 * PAD
    margin = SUBSTEPS - 1
    inside = place[2].astype(jnp.float32)

    def speed(row, spot):
        q = row - SUBSTEPS
        if q < 0:
            return edge[SUBSTEPS - 1 - q, spot, :].astype(jnp.float32)
        return speed_rows[q, spot, :]

    def reward(ctrl, row, spot):
        q = row - SUBSTEPS
        if q < 0:
            return lower_rows[(ctrl - ctrls[0]) * margin - 1 - q, spot, :].astype(jnp.float32)
        return reward_rows[ctrl, q, spot, :]

    def store(ctrl, row, first, size, new):
        fields[0][ctrl, row, pl.ds(PAD + first, size), :] = new * inside if row < SUBSTEPS else new

    sweep(place, coef, ctrls, block, range(1, SUBSTEPS + 1), speed, reward, store)

    def one(ctrl, carry):
        source = fields[0].at[ctrl]
        for substep in range(1, SUBSTEPS):
            last = substep == SUBSTEPS - 1
            for kept in range(2):
                source[substep + kept + SUBSTEPS, pl.ds(PAD, ny), :] = keeps[substep - 1][ctrl, kept]

            def store(ctrl, row, first, size, new, substep=substep, last=last):
                if last:
                    put_max(place, out, row - SUBSTEPS, first, new)
                    return
                new = new * inside if row < SUBSTEPS else new
                fields[substep][row, pl.ds(PAD + first, size), :] = new

            rows = range(1 + substep, SUBSTEPS + 1 + substep)
            sweep(place, coef, [ctrl], source, rows, speed, reward, store)
            source = None if last else fields[substep]
        return carry

    lax.fori_loop(ctrls[0], ctrls[-1] + 1, one, 0)


def pack_kernel(value, speed, reward, edge, far, block, speed_rows, value_sem, speed_sem, near_sem, far_sem):
    place = where_am_i()
    cells, ny = value.shape[:2]
    own = reward.shape[0]
    margin = SUBSTEPS - 1
    copies, later = [], []
    for row in range(SUBSTEPS):
        near = jnp.where(place[1] == 0, row, cells - 1 - row)
        away = jnp.where(place[1] == 0, cells - 1 - row, row)
        copies.append(pltpu.make_async_copy(value.at[near], block.at[row, pl.ds(PAD, ny)], value_sem.at[row]))
        if row < margin:
            copies.append(pltpu.make_async_copy(speed.at[near], speed_rows.at[row], speed_sem.at[row]))
            for ctrl in range(own):
                spot = ctrl * margin + row
                place_near = edge.at[SUBSTEPS + margin + spot]
                later.append(pltpu.make_async_copy(reward.at[ctrl, near], place_near, near_sem.at[spot]))
                later.append(pltpu.make_async_copy(reward.at[ctrl, away], far.at[spot], far_sem.at[spot]))
    for row in range(SUBSTEPS, block.shape[0]):
        real = jnp.where(place[1] == 0, row, cells - 1 - row)
        later.append(pltpu.make_async_copy(value.at[real], block.at[row, pl.ds(PAD, ny)], value_sem.at[row]))
    for copy in copies + later:
        copy.start()
    clear_pads(block, ny)
    for copy in copies:
        copy.wait()
    for row in range(SUBSTEPS):
        edge[row] = block[row, pl.ds(PAD, ny), :].astype(edge.dtype)
    for row in range(margin):
        edge[SUBSTEPS + row] = speed_rows[row].astype(edge.dtype)
    for copy in later:
        copy.wait()


def early_first(coef, block, speed, reward, other, out, *refs, half):
    keeps, (speed_rows, reward_rows), fields = refs[:2], refs[2:4], refs[4:]
    place = where_am_i()
    for field in fields:
        clear_pads(field, speed.shape[1])
    lay_rows(place, speed, reward, other, speed_rows, reward_rows)
    early_march(place, coef, half, block, speed_rows, reward_rows, out, keeps, fields)


def rest_first(coef, first, speed_rows, reward_rows, edge, *refs, half):
    *others, keep_a, keep_b, out, field_a, field_b, block = refs
    place = where_am_i()
    ny = speed_rows.shape[1]
    own = reward_rows.shape[0] // 2
    for field in (field_a.at[pl.ds(own if others else 0, own)], field_b, block):
        clear_pads(field, ny)
    for row in range(SUBSTEPS):
        block[SUBSTEPS - 1 - row, pl.ds(PAD, ny), :] = edge[row].astype(jnp.float32)
    for row in range(2):
        block[SUBSTEPS + row] = first[row]
    if others:
        lower_rows, best = others
        ctrls = range(own, 2 * own)
        for shard in range(out.shape[0]):
            out[shard] = best[shard]
    else:
        lower_rows, ctrls = edge.at[pl.ds(2 * SUBSTEPS - 1, own * (SUBSTEPS - 1))], range(own)
        start_max(out)
    keeps, fields = (keep_a, keep_b), (field_a, field_b)
    rest_march(place, coef, ctrls, edge, lower_rows, block, speed_rows, reward_rows, out, keeps, fields)


def early_later(coef, current, across, speed_rows, reward_rows, out, *refs, half):
    keeps, fields, block = refs[:2], refs[2:4], refs[4]
    place = where_am_i()
    for field in (block, *fields):
        clear_pads(field, speed_rows.shape[1])
    for q in range(half):
        spread(place, current, q, block, q)
    for row in range(SUBSTEPS):
        spread(place, across, SUBSTEPS - 1 - row, block, half + row)
    early_march(place, coef, half, block, speed_rows, reward_rows, out, keeps, fields)


def rest_later(coef, current, beyond, speed_rows, reward_rows, edge, *refs, half):
    edge_other, keeps, out, fields, block, lower_rows = refs[0], refs[1:3], refs[3], refs[4:6], refs[6], refs[7]
    place = where_am_i()
    for field in (block, *fields):
        clear_pads(field, speed_rows.shape[1])
    for row in range(SUBSTEPS):
        spread(place, beyond, row, block, SUBSTEPS - 1 - row)
    for row in range(2):
        spread(place, current, row, block, SUBSTEPS + row)
    lay_lower(edge, edge_other, lower_rows)
    start_max(out)
    ctrls = range(reward_rows.shape[0])
    rest_march(place, coef, ctrls, edge, lower_rows, block, speed_rows, reward_rows, out, keeps, fields)


def body(value, speed, reward, ctrl_set, drift_sets, diffusion_sets):
    own, cells, ny, nz = reward.shape
    count = 2 * own
    slabs, members = lax.axis_size("slab"), lax.axis_size("ctrl")
    chips, half = members // 2, cells // 2
    width = ny // chips
    chip, upper, _ = where_am_i()
    margin = SUBSTEPS - 1
    narrow, wire = jnp.bfloat16, jnp.float16
    both = ("slab", "ctrl")

    def device(s, z, c):
        return s * members + 2 * z + c

    partners = [(i, i ^ 1) for i in range(members)]

    facing, beside = [], []
    for s in range(slabs - 1):
        for z in range(chips):
            c = (s + 1) % 2
            facing += [(device(s, z, c), device(s + 1, z, c)), (device(s + 1, z, c), device(s, z, c))]
            beside += [(device(s, z, 1 - c), device(s + 1, z, c)), (device(s + 1, z, 1 - c), device(s, z, c))]

    whole = pl.BlockSpec(memory_space=pltpu.VMEM)
    scalars = pl.BlockSpec(memory_space=pltpu.SMEM)

    def shape(*dims):
        return jax.ShapeDtypeStruct(dims, jnp.float32)

    def call(kernel, rows, marched, arrays, outs):
        field = pltpu.VMEM((rows, ny + 2 * PAD, nz), jnp.float32)
        scratch = [pltpu.VMEM((count, rows, ny + 2 * PAD, nz), jnp.float32)] + [field] * (SUBSTEPS - 2)
        if kernel is not early_first:
            scratch.append(field)
        if kernel is rest_later:
            scratch.append(pltpu.VMEM((count * margin, ny, nz), narrow))
        return pl.pallas_call(
            functools.partial(kernel, half=half),
            out_shape=outs,
            in_specs=[scalars] + [whole] * len(arrays),
            out_specs=jax.tree.map(lambda _: whole, outs),
            scratch_shapes=scratch,
            compiler_params=pltpu.CompilerParams(vmem_limit_bytes=16 * 2**20),
            cost_estimate=pl.CostEstimate(
                flops=25 * count * marched * ny * nz, bytes_accessed=12 * count * marched * ny * nz, transcendentals=0
            ),
        )(coef, *arrays)

    keeps = [shape(count, 2, ny, nz)] * (SUBSTEPS - 1)

    rows, given = half + SUBSTEPS, half + margin
    other_set = lax.ppermute(ctrl_set, "ctrl", partners)
    other = lax.ppermute(reward, "ctrl", partners)
    anywhere = pl.BlockSpec(memory_space=pl.ANY)
    dma = pltpu.SemaphoreType.DMA
    packed, far, block = pl.pallas_call(
        pack_kernel,
        out_shape=[
            pltpu.VMEM((SUBSTEPS + margin + own * margin, ny, nz), narrow),
            pltpu.VMEM((own * margin, ny, nz), narrow),
            pltpu.VMEM((rows, ny + 2 * PAD, nz), jnp.float32),
        ],
        in_specs=[anywhere] * 3,
        out_specs=[whole] * 3,
        scratch_shapes=[
            pltpu.VMEM((margin, ny, nz), jnp.float32),
            dma((rows,)),
            dma((margin,)),
            dma((own * margin,)),
            dma((own * margin,)),
        ],
    )(value, speed, reward)
    packed, far, other_set = lax.optimization_barrier((packed, far, other_set))
    edge = lax.ppermute(packed, both, facing)
    edge_other = lax.ppermute(far, both, beside)

    sets = jnp.concatenate([ctrl_set, other_set])
    picked = sets[:, None] == jnp.arange(drift_sets.shape[0], dtype=jnp.int32)[None, :]
    pairs = jnp.concatenate([diffusion_sets, drift_sets], axis=1)
    coef = jnp.sum(jnp.where(picked[:, :, None], pairs[None], 0.0), axis=1)

    def from_wire(values):
        return values.astype(jnp.float32) * (1.0 / WIRE_SCALE)

    falling = list(range(chips - 1, 0, -1))
    turned = falling[1:-1] + falling[:1] + falling[-1:]
    odd_core = lax.axis_index("ctrl") % 2

    def reduce(best, orders):
        parts = (best * WIRE_SCALE).astype(wire)
        mine = parts[0]
        for steps_of in zip(*orders):
            pairs = [(2 * z + c, 2 * mate(z, steps_of[c], chips) + c) for z in range(chips) for c in range(2)]
            same = steps_of[0] == steps_of[1]
            part = parts[steps_of[0]] if same else jnp.where(odd_core == 0, parts[steps_of[0]], parts[steps_of[1]])
            mine = jnp.maximum(mine, lax.ppermute(part, "ctrl", pairs))
        return mine

    def gather(mine, orders):
        got = []
        for steps_of in zip(*orders):
            pairs = [(2 * mate(z, steps_of[c], chips) + c, 2 * z + c) for z in range(chips) for c in range(2)]
            got.append(lax.ppermute(mine, "ctrl", pairs))
        pieces = [mine]
        for step in range(1, chips):
            even, odd = got[orders[0].index(step)], got[orders[1].index(step)]
            pieces.append(even if even is odd else jnp.where(odd_core == 0, even, odd))
        return jnp.stack(pieces)

    steps = sum(half + SUBSTEPS - 2 - 2 * k for k in range(SUBSTEPS))
    early_out = [shape(chips, half - SUBSTEPS, width, nz)] + keeps
    rest_out = shape(chips, SUBSTEPS, width, nz)
    rest_rows, rest_steps = 2 * SUBSTEPS + 2, SUBSTEPS * SUBSTEPS

    best, keep_a, keep_b, speed_rows, reward_rows = call(
        early_first,
        rows,
        steps,
        (block, speed, reward, other),
        early_out + [shape(given, ny, nz), shape(count, given, ny, nz)],
    )
    laid, edges = (speed_rows, reward_rows), (edge, edge_other)
    best_rest = call(rest_first, rest_rows, rest_steps // 2, (block, *laid, edge, keep_a, keep_b), rest_out)
    more = (block, *laid, *edges, best_rest, keep_a, keep_b)
    best_rest = call(rest_first, rest_rows, rest_steps // 2, more, rest_out)
    pieces = gather(reduce(jnp.concatenate([best_rest, best], axis=1), (falling, turned)), (falling, turned))

    across = lax.ppermute(pieces[:, -SUBSTEPS:], "ctrl", partners)
    beyond = lax.ppermute(from_wire(pieces[:, :SUBSTEPS]).astype(narrow), both, facing)
    current = from_wire(pieces)
    best, *kept = call(early_later, rows, steps, (current, from_wire(across), *laid), early_out)
    best_rest = call(
        rest_later, rest_rows, rest_steps, (current, beyond, *laid, *edges, *kept), rest_out
    )
    pieces = gather(reduce(jnp.concatenate([best_rest, best], axis=1), (falling, turned)), (falling, turned))

    from_partner = lax.ppermute(pieces, "ctrl", partners)

    def in_order(parts, flipped):
        ordered = [
            lax.dynamic_index_in_dim(parts, mate_step(chip, shard, chips), 0, keepdims=False) for shard in range(chips)
        ]
        block_rows = jnp.concatenate(ordered, axis=1)
        return from_wire(jnp.where(flipped, block_rows[::-1], block_rows))

    result = jnp.zeros((cells, ny, nz), jnp.float32)
    result = lax.dynamic_update_slice_in_dim(result, in_order(pieces, upper == 1), upper * half, axis=0)
    return lax.dynamic_update_slice_in_dim(result, in_order(from_partner, upper == 0), (1 - upper) * half, axis=0)


def solution(mesh):
    in_specs = (
        P("slab", None, None),
        P("slab", None, None),
        P("ctrl", "slab", None, None),
        P("ctrl"),
        P(),
        P(),
    )
    out_specs = P("slab", None, None)
    return jax.shard_map(body, mesh=mesh, in_specs=in_specs, out_specs=out_specs, check_vma=False)
```
